128 devices in a mesh: dp: 8 (over x, y_hi), fsdp: 16 (over y_lo, z, core).
Axes of the slice: x: 4, y: 4 (y_hi: 2, y_lo: 2; y = y_hi * 2 + y_lo), z: 4, core: 2. Of those that a mesh axis runs over, the one named last changes fastest.
Arguments:
- qkv_rows: bfloat16 [8, 16, 8, 64, 4992], P('dp', 'fsdp'), may hold values from -6 to 6
- proj_weight: bfloat16 [3200, 1664], P('fsdp'), may hold values from -0.15625 to 0.15625
- layer_scale: float32 [3200], replicated, may hold values from 0.3 to 3
- out_grad: bfloat16 [8, 16, 320, 3200], P('dp', 'fsdp'), may hold values from -6 to 6
- patch_counts: int32 [8, 16, 8], replicated, may hold values from 16 to 64, as said below
- loader_plan: int32 [8, 16, 8], replicated, may hold values from 0 to 7, as said below
- row_offsets: int32 [8, 16, 8], replicated, may hold values from 0 to 304, as said below
Outputs:
- attn_branch: bfloat16 [8, 16, 320, 3200], P('dp', 'fsdp')
- qkv_grad: bfloat16 [8, 16, 8, 64, 4992], P('dp', 'fsdp')
- weight_grad: float32 [3200, 1664], P('fsdp')
The draws below stay inside these ranges and needn't reach their ends.
Inputs may be any that keep to these rules, and one draw needn't show every extreme that they name: `patch_counts`: the 8 images of each owner pair up so that the two counts of a pair sum to 80; in some owner an image has 64 patches. For each column f and image k, (loader_plan[e, f, k] - e) mod 8 is the same for every owner e and differs between images, so each loader holds one image of every owner in its column. The images of one owner occupy the disjoint row ranges from row_offsets to row_offsets + patch_counts - 1 and together fill all 320 rows.
All inputs are finite; a program needn't handle non-finite values.
Results may differ from the reference program's by a relative error of at most 0.015.
Values may be sent and summed in bfloat16 or wider, within the bound.
A program may use at most 192 MiB of HBM per device.

```python
import math
import jax
import jax.numpy as jnp
from jax import lax

D = 3200
HEADS = 13
HEAD = 128
MAXP = 64
MINP = 16
IMGS = 8
OWN = 320
N_DP = 8
N_FSDP = 16


def owner_counts(key):
    key = jax.random.fold_in(key, 17)
    first_key, pick_key, mix_key = jax.random.split(key, 3)
    owners_all = N_DP * N_FSDP
    first_half = jax.random.randint(first_key, (owners_all, IMGS // 2), MINP, MAXP + 1)
    chosen = jax.random.randint(pick_key, (), 0, owners_all)
    forced = (jnp.arange(owners_all) == chosen)[:, None] & (jnp.arange(IMGS // 2) == 0)[None, :]
    first_half = jnp.where(forced, MAXP, first_half)
    paired = jnp.concatenate([first_half, MINP + MAXP - first_half], axis=1)
    mixers = jax.vmap(lambda part_key: jax.random.permutation(part_key, IMGS))(jax.random.split(mix_key, owners_all))
    return jnp.take_along_axis(paired, mixers, axis=1).reshape(N_DP, N_FSDP, IMGS).astype(jnp.int32)


def draw_patch_counts(key, part):
    return owner_counts(key)


def draw_row_offsets(key, part):
    counts_now = owner_counts(key)
    key = jax.random.fold_in(key, 5)
    orders = jax.vmap(lambda part_key: jax.random.permutation(part_key, IMGS))(jax.random.split(key, N_DP * N_FSDP))
    orders = orders.reshape(N_DP, N_FSDP, IMGS)
    positions = jnp.arange(IMGS, dtype=jnp.int32)
    matched = (orders[..., :, None] == positions[None, None, None, :]).astype(jnp.int32)
    ranks = jnp.sum(matched * positions[None, None, :, None], axis=2)
    earlier = (ranks[..., :, None] < ranks[..., None, :]).astype(jnp.int32)
    return jnp.sum(counts_now[..., :, None] * earlier, axis=2).astype(jnp.int32)


def draw_loader_plan(key, part):
    key = jax.random.fold_in(key, 3)
    shifts = jax.vmap(lambda part_key: jax.random.permutation(part_key, N_DP))(jax.random.split(key, N_FSDP))
    owners = jnp.arange(N_DP, dtype=jnp.int32)[:, None, None]
    return ((owners + shifts[None, :, :]) % N_DP).astype(jnp.int32)


def draw_qkv_rows(key, part):
    key = jax.random.fold_in(key, 7)
    base_key = jax.random.fold_in(key, 0)
    feature = HEADS * HEAD
    shape = (N_DP, N_FSDP, IMGS, MAXP, 3 * feature)
    values = jnp.clip(jax.random.normal(base_key, shape, jnp.float32), -5.0, 5.0)
    return values.astype(jnp.bfloat16)


def spiked(entries, rng, source, target, blocks, factor):
    owner, partner = [(jnp.arange(entries.shape[axis_at]) // (entries.shape[axis_at] // blocks)).reshape([-1 if axis == axis_at else 1 for axis in range(entries.ndim)]) for axis_at in (source, target)]
    chosen = jax.random.permutation(rng, blocks)[partner]
    strong = (owner == chosen) | (owner == (partner + blocks // 2) % blocks)
    return jnp.where(strong, factor * entries, entries)


def level_of(rng, dims, cuts, low, high):
    gain, own = 1.0, jax.random.fold_in(rng, 6)
    for axis_at, shards_of in cuts:
        heights = jnp.exp(jax.random.uniform(jax.random.fold_in(own, axis_at), (shards_of,), jnp.float32, low / len(cuts), high / len(cuts)))
        gain = gain * jnp.repeat(heights, dims[axis_at] // shards_of).reshape([-1 if axis == axis_at else 1 for axis in range(len(dims))])
    return gain


def centred(own_key, shape, scale, bound, cuts=(), kind=jnp.bfloat16):
    array = jax.random.normal(own_key, shape, jnp.float32) * scale
    if len(cuts) > 0:
        array = level_of(own_key, shape, cuts, -0.22, 0.18) * array
    return jnp.clip(array, min=-bound, max=bound).astype(kind)


def bell_draw_with(stream_key, dims, scale, reach, shards, heavy, kind=jnp.bfloat16):
    drawn = scale * jax.random.normal(stream_key, dims, jnp.float32)
    if shards:
        drawn = drawn * level_of(stream_key, dims, shards, -0.22, 0.18)
    return jnp.clip(spiked(drawn, jax.random.fold_in(stream_key, 3), *heavy), -reach, reach).astype(kind)


def setup_inputs(seed: int = 0) -> dict:
    splits = jax.random.split(jax.random.key(seed), 8)
    qkv_rows = draw_qkv_rows(jax.random.fold_in(splits[7], 71), 0)
    proj_weight = centred(splits[1], (D, HEADS * HEAD), (HEADS * HEAD) ** -0.5, 0.15625, ((0, 16),))
    layer_scale = jnp.clip(jnp.exp(jax.random.uniform(splits[2], (D,), jnp.float32, math.log(0.3), math.log(3.0))), 0.3, 3.0)
    out_grad = bell_draw_with(splits[3], (N_DP, N_FSDP, OWN, D), 1.0, 6.0, ((0, 8), (1, 16)), (1, 3, 16, 2.0))
    patch_counts = draw_patch_counts(jax.random.fold_in(splits[7], 71), 0)
    loader_plan = draw_loader_plan(jax.random.fold_in(splits[7], 71), 0)
    row_offsets = draw_row_offsets(jax.random.fold_in(splits[7], 71), 0)
    return dict(qkv_rows=qkv_rows, proj_weight=proj_weight, layer_scale=layer_scale, out_grad=out_grad, patch_counts=patch_counts, loader_plan=loader_plan, row_offsets=row_offsets)


MASKED = -1e+30

def split_heads(block):
    feature = block.shape[-1] // 3
    shape_lead = block.shape[:-1]
    queries = block[..., :feature].reshape(shape_lead + (HEADS, HEAD))
    key_rows = block[..., feature:2 * feature].reshape(shape_lead + (HEADS, HEAD))
    value_rows = block[..., 2 * feature:].reshape(shape_lead + (HEADS, HEAD))
    return (queries, key_rows, value_rows)

def attend(block, groups):
    queries, key_rows, value_rows = split_heads(block)
    inv_scale = 1.0 / math.sqrt(HEAD)
    scores = jnp.einsum('bqhd,bkhd->bhqk', queries.astype(jnp.float32), key_rows.astype(jnp.float32)) * inv_scale
    allowed = (groups[:, :, None] == groups[:, None, :]) & (groups[:, None, :] >= 0)
    scores = jnp.where(allowed[:, None], scores, MASKED)
    row_max = lax.optimization_barrier(jnp.max(scores, axis=-1, keepdims=True))
    expo_rows = jnp.exp(scores - row_max)
    soft = expo_rows / lax.optimization_barrier(jnp.sum(expo_rows, axis=-1, keepdims=True))
    soft_low = soft.astype(jnp.bfloat16)
    mixed_heads = jnp.einsum('bhqk,bkhd->bqhd', soft_low.astype(jnp.float32), value_rows.astype(jnp.float32))
    live_rows = (groups >= 0)[:, :, None, None]
    attn_out = jnp.where(live_rows, mixed_heads, 0.0).astype(jnp.bfloat16)
    attn_out = attn_out.reshape(block.shape[:-1] + (HEADS * HEAD,))
    return (attn_out, soft, soft_low)

def attend_back(block, soft, soft_low, attn_out, grad_out):
    queries, key_rows, value_rows = split_heads(block)
    inv_scale = 1.0 / math.sqrt(HEAD)
    shape_lead = block.shape[:-1]
    grad_heads = grad_out.reshape(shape_lead + (HEADS, HEAD)).astype(jnp.float32)
    out_heads = attn_out.reshape(shape_lead + (HEADS, HEAD)).astype(jnp.float32)
    grad_value = jnp.einsum('bhqk,bqhd->bkhd', soft_low.astype(jnp.float32), grad_heads).astype(jnp.bfloat16)
    grad_soft = jnp.einsum('bqhd,bkhd->bhqk', grad_heads, value_rows.astype(jnp.float32))
    delta = lax.optimization_barrier(jnp.sum(grad_heads * out_heads, axis=-1))
    grad_score = soft * (grad_soft - jnp.transpose(delta, (0, 2, 1))[..., None])
    score_low = grad_score.astype(jnp.bfloat16).astype(jnp.float32)
    grad_query = (jnp.einsum('bhqk,bkhd->bqhd', score_low, key_rows.astype(jnp.float32)) * inv_scale).astype(jnp.bfloat16)
    grad_key = (jnp.einsum('bhqk,bqhd->bkhd', score_low, queries.astype(jnp.float32)) * inv_scale).astype(jnp.bfloat16)
    width_all = HEADS * HEAD
    return jnp.concatenate([grad_query.reshape(shape_lead + (width_all,)), grad_key.reshape(shape_lead + (width_all,)), grad_value.reshape(shape_lead + (width_all,))], axis=-1)

def reference(qkv_rows, proj_weight, layer_scale, out_grad, patch_counts, loader_plan, row_offsets):
    slot_pos = jnp.arange(MAXP, dtype=jnp.int32)
    image_ids = jnp.arange(IMGS, dtype=jnp.int32)
    row_ids = jnp.arange(OWN, dtype=jnp.int32)

    def one_owner(total, owner_index):
        dp_pos = owner_index // N_FSDP
        fsdp_pos = owner_index % N_FSDP
        sources = loader_plan[dp_pos, fsdp_pos]
        sizes_here = patch_counts[dp_pos, fsdp_pos]
        starts = row_offsets[dp_pos, fsdp_pos]
        images = qkv_rows[sources, fsdp_pos, image_ids]
        slot_valid = slot_pos[None, :] < sizes_here[:, None]
        groups = jnp.where(slot_valid, 0, -1).astype(jnp.int32)
        attn_out, soft, soft_low = attend(images, groups)
        attended = attn_out.reshape(IMGS * MAXP, HEADS * HEAD)
        projected = lax.dot_general(attended, proj_weight, (((1,), (1,)), ((), ())), preferred_element_type=jnp.float32)
        branch_slots = (layer_scale * projected).astype(jnp.bfloat16)
        inside = ((row_ids[:, None] >= starts[None, :]) & (row_ids[:, None] < (starts + sizes_here)[None, :])).astype(jnp.int32)
        segment = lax.optimization_barrier(jnp.sum(inside * image_ids[None, :], axis=1))
        row_base = lax.optimization_barrier(jnp.sum(inside * starts[None, :], axis=1))
        packed = branch_slots[(segment * MAXP + row_ids - row_base).astype(jnp.int32)]
        back_index = jnp.clip(starts[:, None] + slot_pos[None, :], 0, OWN - 1).astype(jnp.int32)
        cot_slots = out_grad[dp_pos, fsdp_pos][back_index]
        scaled = (cot_slots.astype(jnp.float32) * layer_scale).astype(jnp.bfloat16)
        scaled = jnp.where(slot_valid[..., None], scaled, jnp.zeros_like(scaled)).reshape(IMGS * MAXP, D)
        grad_attended = jnp.dot(scaled, proj_weight, preferred_element_type=jnp.float32).astype(jnp.bfloat16)
        total = total + lax.dot_general(scaled, attended, (((0,), (0,)), ((), ())), preferred_element_type=jnp.float32)
        grads = attend_back(images, soft, soft_low, attn_out, grad_attended.reshape(IMGS, MAXP, HEADS * HEAD))
        return (total, (packed, grads))
    start_total = jnp.zeros((D, HEADS * HEAD), jnp.float32)
    total, (packed, grads) = lax.scan(one_owner, start_total, jnp.arange(N_DP * N_FSDP, dtype=jnp.int32))
    attn_branch = packed.reshape(N_DP, N_FSDP, OWN, D)
    grads = grads.reshape(N_DP, N_FSDP, IMGS, MAXP, 3 * HEADS * HEAD)
    fsdp_grid = jnp.arange(N_FSDP, dtype=jnp.int32)[None, :, None]
    image_grid = jnp.arange(IMGS, dtype=jnp.int32)[None, None, :]
    qkv_grad = jnp.zeros(qkv_rows.shape, jnp.bfloat16).at[loader_plan, fsdp_grid, image_grid].set(grads)
    return (attn_branch, qkv_grad, total)
```

```python
import math

import jax
import jax.numpy as jnp
from jax import lax
from jax.sharding import PartitionSpec as P

HEADS = 13
HEAD = 128


MASKED = -1e30


def split_heads(block):
    feature = block.shape[-1] // 3
    shape_lead = block.shape[:-1]
    queries = block[..., :feature].reshape(shape_lead + (HEADS, HEAD))
    key_rows = block[..., feature : 2 * feature].reshape(shape_lead + (HEADS, HEAD))
    value_rows = block[..., 2 * feature :].reshape(shape_lead + (HEADS, HEAD))
    return (queries, key_rows, value_rows)


def attend(block, groups):
    queries, key_rows, value_rows = split_heads(block)
    inv_scale = 1.0 / math.sqrt(HEAD)
    scores = (
        jnp.einsum("bqhd,bkhd->bhqk", queries, key_rows, preferred_element_type=jnp.float32)
        * inv_scale
    )
    allowed = (groups[:, :, None] == groups[:, None, :]) & (groups[:, None, :] >= 0)
    scores = jnp.where(allowed[:, None], scores, MASKED)
    row_max = jnp.max(scores, axis=-1, keepdims=True)
    expo_rows = jnp.exp(scores - row_max)
    soft = expo_rows / jnp.sum(expo_rows, axis=-1, keepdims=True)
    soft_low = soft.astype(jnp.bfloat16)
    mixed_heads = jnp.einsum(
        "bhqk,bkhd->bqhd", soft_low, value_rows, preferred_element_type=jnp.float32
    )
    live_rows = (groups >= 0)[:, :, None, None]
    attn_out = jnp.where(live_rows, mixed_heads, 0.0).astype(jnp.bfloat16)
    attn_out = attn_out.reshape(block.shape[:-1] + (HEADS * HEAD,))
    return (attn_out, soft, soft_low)


def attend_back(block, soft, soft_low, attn_out, grad_out):
    queries, key_rows, value_rows = split_heads(block)
    inv_scale = 1.0 / math.sqrt(HEAD)
    shape_lead = block.shape[:-1]
    grad_heads = grad_out.reshape(shape_lead + (HEADS, HEAD))
    out_heads = attn_out.reshape(shape_lead + (HEADS, HEAD))
    grad_value = jnp.einsum(
        "bhqk,bqhd->bkhd", soft_low, grad_heads, preferred_element_type=jnp.float32
    ).astype(jnp.bfloat16)
    grad_soft = jnp.einsum(
        "bqhd,bkhd->bhqk", grad_heads, value_rows, preferred_element_type=jnp.float32
    )
    delta = jnp.sum(grad_heads.astype(jnp.float32) * out_heads.astype(jnp.float32), axis=-1)
    grad_score = soft * (grad_soft - jnp.transpose(delta, (0, 2, 1))[..., None])
    score_low = grad_score.astype(jnp.bfloat16)
    grad_query = (
        jnp.einsum("bhqk,bkhd->bqhd", score_low, key_rows, preferred_element_type=jnp.float32)
        * inv_scale
    ).astype(jnp.bfloat16)
    grad_key = (
        jnp.einsum("bhqk,bqhd->bkhd", score_low, queries, preferred_element_type=jnp.float32)
        * inv_scale
    ).astype(jnp.bfloat16)
    width_all = HEADS * HEAD
    return jnp.concatenate(
        [
            grad_query.reshape(shape_lead + (width_all,)),
            grad_key.reshape(shape_lead + (width_all,)),
            grad_value.reshape(shape_lead + (width_all,)),
        ],
        axis=-1,
    )


def project(attended, weights, layer_scale):
    projected = lax.dot_general(
        attended, weights, (((1,), (1,)), ((), ())), preferred_element_type=jnp.float32
    )
    return (layer_scale * projected).astype(jnp.bfloat16)


def per_device(
    qkv_rows, proj_weight, layer_scale, out_grad, patch_counts, loader_plan, row_offsets
):
    dp_count = lax.axis_size("dp")
    dp_index = lax.axis_index("dp")
    column = lax.axis_index("fsdp")
    col_plan = lax.dynamic_index_in_dim(loader_plan, column, 1, keepdims=False)
    col_counts = lax.dynamic_index_in_dim(patch_counts, column, 1, keepdims=False)
    col_offsets = lax.dynamic_index_in_dim(row_offsets, column, 1, keepdims=False)
    my_plan = lax.dynamic_index_in_dim(col_plan, dp_index, 0, keepdims=False)
    my_counts = lax.dynamic_index_in_dim(col_counts, dp_index, 0, keepdims=False)
    my_offsets = lax.dynamic_index_in_dim(col_offsets, dp_index, 0, keepdims=False)
    slot_data = qkv_rows[0, 0]
    grad_rows = out_grad[0, 0]
    images_count, slot_len = slot_data.shape[:2]
    own_rows = grad_rows.shape[0]
    slot_pos = jnp.arange(slot_len, dtype=jnp.int32)
    image_ids = jnp.arange(images_count, dtype=jnp.int32)
    owner_ids = jnp.arange(dp_count, dtype=jnp.int32)
    row_ids = jnp.arange(own_rows, dtype=jnp.int32)
    slot_of_owner = col_plan == dp_index
    loader_counts = jnp.sum(jnp.where(slot_of_owner, col_counts, 0), axis=0)
    image_of_loader = my_plan[None, :] == owner_ids[:, None]
    offset_from = jnp.sum(jnp.where(image_of_loader, my_offsets[None, :], 0), axis=1)
    count_from = jnp.sum(jnp.where(image_of_loader, my_counts[None, :], 0), axis=1)
    source_row = jnp.where(
        slot_pos[None, :] < count_from[:, None], offset_from[:, None] + slot_pos[None, :], -1
    ).reshape(-1)
    pack = (row_ids[:, None] == source_row[None, :]).astype(jnp.bfloat16)
    groups = jnp.where(slot_pos[None, :] < loader_counts[:, None], 0, -1)

    weights = lax.all_gather(proj_weight, "fsdp", axis=0, tiled=True)
    attn_out, soft, soft_low = attend(slot_data, groups)
    swap = slot_of_owner.astype(jnp.bfloat16)
    width = attn_out.shape[-1]
    outgoing = jnp.dot(swap, attn_out.reshape(images_count, -1))
    incoming = lax.all_to_all(
        outgoing.reshape(dp_count, slot_len, width), "dp", split_axis=0, concat_axis=0, tiled=True
    )
    attended = jnp.dot(pack, incoming.reshape(-1, width))
    scaled = (grad_rows.astype(jnp.float32) * layer_scale).astype(jnp.bfloat16)
    grad_attended = jnp.dot(scaled, weights, preferred_element_type=jnp.float32).astype(
        jnp.bfloat16
    )
    back_send = jnp.dot(pack.T, grad_attended)
    returned = lax.all_to_all(
        back_send.reshape(dp_count, slot_len, width), "dp", split_axis=0, concat_axis=0, tiled=True
    )
    grad_slots = jnp.dot(swap.T, returned.reshape(dp_count, -1)).reshape(
        images_count, slot_len, width
    )
    branch_rows = project(attended, weights, layer_scale)
    shard_sum = lax.psum_scatter(
        lax.dot_general(
            scaled, attended, (((0,), (0,)), ((), ())), preferred_element_type=jnp.float32
        ).astype(jnp.bfloat16),
        "fsdp",
        scatter_dimension=0,
        tiled=True,
    )
    weight_grad = lax.psum(shard_sum.astype(jnp.float32), "dp")
    grad_patches = attend_back(slot_data, soft, soft_low, attn_out, grad_slots)
    valid = slot_pos[None, :] < loader_counts[:, None]
    grad_patches = jnp.where(valid[..., None], grad_patches, jnp.zeros((), jnp.bfloat16))
    return (branch_rows[None, None], grad_patches[None, None], weight_grad)


def solution(mesh):
    in_specs = (
        P("dp", "fsdp", None, None, None),
        P("fsdp", None),
        P(),
        P("dp", "fsdp", None, None),
        P(),
        P(),
        P(),
    )
    out_specs = (P("dp", "fsdp", None, None), P("dp", "fsdp", None, None, None), P("fsdp", None))
    return jax.shard_map(
        per_device, mesh=mesh, in_specs=in_specs, out_specs=out_specs, check_vma=False
    )
```

```python
import math

import jax
import jax.numpy as jnp
from jax import lax
from jax.experimental import pallas as pl
from jax.experimental.pallas import tpu as pltpu
from jax.sharding import PartitionSpec as P

HEADS = 13
HEAD = 128
WIDTH = HEADS * HEAD
D = 3200
IMGS = 8
MAXP = 64
OWN = 320
SHARD = 200
PADDED = 208
HALF = 8 * PADDED
BLOCK = 896
SECOND = WIDTH - BLOCK
CUT = 96
MASKED = -1e30
MESH = pl.DeviceIdType.MESH
INV_SCALE = 1.0 / math.sqrt(HEAD)
F32 = jnp.float32
BF16 = jnp.bfloat16

NN = (((1,), (0,)), ((), ()))
NT = (((1,), (1,)), ((), ()))
TN = (((0,), (0,)), ((), ()))


def mm(a, b, dims=NN):
    return lax.dot_general(a, b, dims, preferred_element_type=F32)


def by_columns(body):
    @pl.loop(0, WIDTH // 256)
    def _(n):
        body(pl.multiple_of(n * 256, 128), 256)

    body(WIDTH - WIDTH % 256, WIDTH % 256)


def spread_tile(tile):
    first = tile * 128
    group = first // PADDED
    inside = first % PADDED
    start = lax.min((group * SHARD + lax.min(inside, SHARD)) // 128, D // 128 - 2)
    place = first + lax.broadcasted_iota(jnp.int32, (256, 128), 1)
    source = start * 128 + lax.broadcasted_iota(jnp.int32, (256, 128), 0)
    groups = group + (place >= (group + 1) * PADDED).astype(jnp.int32)
    local = place - groups * PADDED
    hit = (source == groups * SHARD + local) & (local < SHARD)
    return start * 128, jnp.where(hit, 1.0, 0.0).astype(BF16)


def compact_tile(tile):
    first = tile * 128
    group = first // SHARD
    start = lax.min((first + group * (PADDED - SHARD)) // 128, 2 * HALF // 128 - 3)
    place = first + lax.broadcasted_iota(jnp.int32, (384, 128), 1)
    source = start * 128 + lax.broadcasted_iota(jnp.int32, (384, 128), 0)
    groups = group + (place >= (group + 1) * SHARD).astype(jnp.int32)
    hit = source == place + groups * (PADDED - SHARD)
    return start * 128, jnp.where(hit, 1.0, 0.0).astype(BF16)


def fused(
    meta, shard_hbm, qkv_hbm, grad_hbm, scale, scale_pad, source_row, source_col,
    branch_hbm, qkv_grad_hbm, weight_grad_hbm,
    wv, wp, wh, qkv, sc, sp, sx, att_send, att_recv, aa, soft_keep,
    gh, relay, direct, total, relay2, direct2, summed, ysum, mixed, final, wout,
    ga_own, ga_send, ga_recv, back_send, back_recv, bp, bx,
    in_sem, w0s, w0r, w1s, w1r, a2s, a2r, cs, cr, g1s, g1r, g2s, g2r, ys, yr, fs, fr, b2s, b2r, out_sem,
):
    d = lax.axis_index("dp")
    f = lax.axis_index("fsdp")
    c = f % 2
    z = (f // 2) % 4
    yl = f // 8
    x = d // 2
    y = (d % 2) * 2 + yl

    def at(px, py, pz, pc):
        px, py, pz = (px + 4) % 4, (py + 4) % 4, (pz + 4) % 4
        return (px * 2 + py // 2, ((py % 2) * 4 + pz) * 2 + pc)

    def remote(src, dst, send, recv, dev):
        return pltpu.make_async_remote_copy(
            src_ref=src, dst_ref=dst, send_sem=send, recv_sem=recv, device_id=dev, device_id_type=MESH
        )

    partner = at(x, y, z, 1 - c)

    load_w = pltpu.make_async_copy(shard_hbm, wv, in_sem.at[0])
    load_q = pltpu.make_async_copy(qkv_hbm, qkv, in_sem.at[1])
    load_g = pltpu.make_async_copy(grad_hbm, sc, in_sem.at[2])
    load_w.start()
    load_q.start()
    load_g.start()

    barrier = pltpu.get_barrier_semaphore()
    peers = []
    for step in range(1, 8):
        other = (d + step) % 8
        peers += [(other, f), (other, f + 1 - 2 * c)]
    peers += [partner, at(x, y, z + 1, c), at(x, y, z - 1, c)]
    for sign in (1, -1):
        peers += [at(x, y + sign, z, 0), at(x, y + sign, z, 1)]
    for peer in peers:
        pl.semaphore_signal(barrier, inc=1, device_id=peer, device_id_type=MESH)
    load_w.wait()
    wp[0:192, :] = wv[0:192, :]
    wp[192:208, :] = jnp.concatenate(
        [wv[192:200, :].astype(F32), jnp.zeros((8, WIDTH), F32)], axis=0
    ).astype(BF16)
    pl.semaphore_wait(barrier, len(peers))

    def w_rows(pz, k):
        return wh.at[pl.ds(pl.multiple_of((((pz + 4) % 4) * 2 + k) * PADDED, 16), PADDED), :]

    w_y = remote(wp, w_rows(z, c), w0s.at[0], w0r.at[c], at(x, y + 1 - 2 * c, z, yl))
    w_c = remote(wp, w_rows(z, c), w0s.at[1], w0r.at[c], partner)
    w_l = pltpu.make_async_copy(wp, w_rows(z, c), w0s.at[1])
    w_y.start()

    @pl.when(c == yl)
    def _():
        w_l.start()

    @pl.when(c != yl)
    def _():
        w_c.start()

    load_q.wait()

    def att_copy(i):
        owner = (d + 1 + i) % 8
        return remote(att_send.at[owner], att_recv.at[d], a2s.at[i], a2r.at[i], (owner, f))

    @pl.loop(0, IMGS)
    def _(i):
        owner = (d + 1 + i) % 8
        slot = meta[0, owner]
        count = meta[1, owner]
        live = lax.broadcasted_iota(jnp.int32, (MAXP, MAXP), 1) < count
        for h in range(HEADS):
            cols = slice(h * HEAD, (h + 1) * HEAD)
            q = qkv[slot, :, cols]
            k = qkv[slot, :, WIDTH + h * HEAD : WIDTH + (h + 1) * HEAD]
            v = qkv[slot, :, 2 * WIDTH + h * HEAD : 2 * WIDTH + (h + 1) * HEAD]
            s = jnp.where(live, mm(q, k, NT) * INV_SCALE, MASKED)
            e = jnp.exp(s - jnp.max(s, axis=-1, keepdims=True))
            soft = e / jnp.sum(e, axis=-1, keepdims=True)
            soft_keep[owner, h] = soft
            att_send[owner, :, cols] = mm(soft.astype(BF16), v).astype(BF16)

        @pl.when(i < 7)
        def _():
            att_copy(i).start()

    att_recv[d] = att_send[d]

    for k in range(2):
        @pl.when((c != yl) | (c != k))
        def _():
            remote(wp, w_rows(z, k), w0s.at[0], w0r.at[k], partner).wait_recv()

    @pl.when(c == yl)
    def _():
        w_l.wait()

    up, down = at(x, y, z + 1, c), at(x, y, z - 1, c)
    w1 = [
        remote(w_rows(z, 0), w_rows(z, 0), w1s.at[0], w1r.at[0], up),
        remote(w_rows(z, 1), w_rows(z, 1), w1s.at[1], w1r.at[1], down),
        remote(w_rows(z, 1), w_rows(z, 1), w1s.at[2], w1r.at[2], up),
        remote(w_rows(z, 0), w_rows(z, 0), w1s.at[3], w1r.at[3], down),
    ]
    for copy in w1:
        copy.start()
    w2 = [
        remote(w_rows(z - 1, 0), w_rows(z - 1, 0), w1s.at[4], w1r.at[4], up),
        remote(w_rows(z + 1, 1), w_rows(z + 1, 1), w1s.at[5], w1r.at[5], down),
    ]

    load_g.wait()

    @pl.loop(0, OWN // 16)
    def _(r):
        rows = pl.ds(pl.multiple_of(r * 16, 16), 16)
        sc[rows, :] = (sc[rows, :].astype(F32) * scale[...]).astype(BF16)

    own_rows = pl.ds(pl.multiple_of(c * OWN, 16), OWN)
    other_rows = pl.ds(pl.multiple_of((1 - c) * OWN, 16), OWN)

    @pl.loop(0, HALF // 128)
    def _(t):
        start, pick = spread_tile((1 - c) * (HALF // 128) + t)
        window = sc[:, pl.ds(pl.multiple_of(start, 128), 256)]
        sx[:, pl.ds(pl.multiple_of(t * 128, 128), 128)] = mm(window, pick).astype(BF16)

    send_sx = remote(sx, sp.at[own_rows, :], cs.at[0], cr.at[0], partner)
    send_sx.start()

    @pl.loop(0, HALF // 128)
    def _(t):
        start, pick = spread_tile(c * (HALF // 128) + t)
        window = sc[:, pl.ds(pl.multiple_of(start, 128), 256)]
        sp[own_rows, pl.ds(pl.multiple_of(t * 128, 128), 128)] = mm(window, pick).astype(BF16)

    for i in range(7):
        source = (d + 7 - i) % 8
        remote(att_send.at[source], att_recv.at[source], a2s.at[i], a2r.at[i], partner).wait_recv()
    pack = jnp.where(
        lax.broadcasted_iota(jnp.int32, (OWN, IMGS * MAXP), 0) == source_row[...], 1.0, 0.0
    ).astype(BF16)

    def pack_columns(start, size):
        got = att_recv[:, :, pl.ds(start, size)].reshape(IMGS * MAXP, size)
        aa[own_rows, pl.ds(start, size)] = mm(pack, got).astype(BF16)

    by_columns(pack_columns)
    send_aa = remote(aa.at[own_rows, :], aa.at[own_rows, :], cs.at[1], cr.at[1], partner)
    send_aa.start()
    remote(sx, sp.at[other_rows, :], cs.at[0], cr.at[0], partner).wait_recv()
    remote(aa.at[other_rows, :], aa.at[other_rows, :], cs.at[1], cr.at[1], partner).wait_recv()

    @pl.loop(0, HALF // 128)
    def _(t):
        rows = pl.ds(pl.multiple_of(t * 128, 128), 128)
        part = mm(sp[:, rows], aa[...], TN)
        gh[0, rows, :] = part[:, :BLOCK].astype(BF16)
        gh[1, rows, :] = part[:, SECOND:].astype(BF16)

    def block(first, second):
        first, second = (first + 4) % 4, (second + 4) % 4
        pz = first * (1 - c) + second * c
        kh = second * (1 - c) + first * c
        return kh % 2, pl.ds(pl.multiple_of((pz * 2 + kh // 2) * PADDED, 16), PADDED)

    p1 = z * (1 - c) + x * c
    p2 = x * (1 - c) + z * c
    right1, left1 = at(x + c, y, z + 1 - c, c), at(x - c, y, z - 1 + c, c)
    right2, left2 = at(x + 1 - c, y, z + c, c), at(x - 1 + c, y, z - c, c)

    def g1(first, j, dst, sem, dev):
        h, rows = block(first, j)
        return remote(gh.at[h, rows, :], dst, g1s.at[sem], g1r.at[sem], dev)

    s1 = [g1(p1 + 2, j, relay.at[0, j], j, right1) for j in (0, 1)]
    s1 += [g1(p1 + 2, j, relay.at[1, j - 2], j, left1) for j in (2, 3)]
    s1 += [g1(p1 + 1, j, direct.at[0, j], 4 + j, right1) for j in (2, 3)]
    s1 += [g1(p1 - 1, j, direct.at[1, j], 8 + j, left1) for j in (0, 1)]
    for copy in (s1[0], s1[2], s1[1], s1[3], s1[4], s1[6], s1[5], s1[7]):
        copy.start()
    r1 = [g1(p1 + 1, j, direct.at[0, j], 4 + j, right1) for j in (0, 1)]
    r1 += [g1(p1 - 1, j, direct.at[1, j], 8 + j, left1) for j in (2, 3)]

    w1[0].wait_recv()
    w2[0].start()
    w1[1].wait_recv()
    w2[1].start()

    def add_rows(rows, body):
        @pl.loop(0, rows // 16)
        def _(r):
            body(pl.multiple_of(r * 16, 16))

    for n, j in enumerate((0, 2, 1, 3)):
        side, place = (0, p1 + 1) if j < 2 else (1, p1 - 1)
        s1[j].wait_recv()
        h, rows = block(place, j)
        base = rows.start

        def add_relay(r, h=h, base=base, side=side, j=j):
            here = pl.ds(pl.multiple_of(base + r, 16), 16)
            gh[h, here, :] = (
                gh[h, here, :].astype(F32) + relay[side, j % 2, pl.ds(r, 16), :].astype(F32)
            ).astype(BF16)

        add_rows(PADDED, add_relay)
        r1[j].start()

    w1[2].wait_recv()
    w1[3].wait_recv()
    w2[0].wait_recv()
    w2[1].wait_recv()

    def grad_columns(start, size):
        cols = pl.ds(start, size)
        ga_send[:, cols] = mm(sp[other_rows, :], wh[:, cols])
        ga_own[:, cols] = mm(sp[own_rows, :], wh[:, cols])

    by_columns(grad_columns)
    send_ga = remote(ga_send, ga_recv, cs.at[2], cr.at[2], partner)
    send_ga.start()
    send_ga.wait_recv()
    unpack = jnp.where(
        lax.broadcasted_iota(jnp.int32, (IMGS * MAXP, OWN), 1) == source_col[...], 1.0, 0.0
    ).astype(BF16)

    def unpack_columns(start, size):
        cols = pl.ds(start, size)
        grad = (ga_own[:, cols] + ga_recv[:, cols]).astype(BF16)
        back_send[:, :, cols] = mm(unpack, grad).astype(BF16).reshape(IMGS, MAXP, size)

    by_columns(unpack_columns)

    def back_copy(i):
        loader = (d + 1 + i) % 8
        return remote(back_send.at[loader], back_recv.at[d], b2s.at[i], b2r.at[i], (loader, f))

    for i in range(7):
        back_copy(i).start()
    back_recv[d] = back_send[d]

    for j in range(4):
        (s1[4 + j - 2] if j >= 2 else r1[j]).wait_recv()
        (s1[6 + j] if j < 2 else r1[j]).wait_recv()
        h, rows = block(p1, j)
        base = rows.start

        def add_first(r, h=h, base=base, j=j):
            here = pl.ds(r, 16)
            total[j, here, :] = (
                gh[h, pl.ds(pl.multiple_of(base + r, 16), 16), :].astype(F32)
                + direct[0, j, here, :].astype(F32)
                + direct[1, j, here, :].astype(F32)
            ).astype(BF16)

        add_rows(PADDED, add_first)

    low, high = pl.ds(0, CUT), pl.ds(CUT, PADDED - CUT)

    def g2(place, rows, dst, sem, dev):
        return remote(total.at[(place + 4) % 4, rows, :], dst, g2s.at[sem], g2r.at[sem], dev)

    s2 = [
        g2(p2 + 2, low, relay2.at[low, :], 0, right2),
        g2(p2 + 2, high, relay2.at[high, :], 1, left2),
        g2(p2 + 1, high, direct2.at[0, high, :], 2, right2),
        g2(p2 - 1, low, direct2.at[1, low, :], 3, left2),
    ]
    r2 = [
        g2(p2 + 1, low, direct2.at[0, low, :], 4, right2),
        g2(p2 - 1, high, direct2.at[1, high, :], 5, left2),
    ]
    for copy in s2:
        copy.start()

    @pl.loop(0, HALF // 128)
    def _(t):
        rows = pl.ds(pl.multiple_of(t * 128, 128), 128)
        there = pl.ds(pl.multiple_of(c * HALF + t * 128, 128), 128)
        factor = scale_pad[:, there]
        weights = wh[rows, :]
        bx[:, rows] = (factor * mm(aa[other_rows, :], weights, NT)).astype(BF16)
        bp[:, there] = (factor * mm(aa[own_rows, :], weights, NT)).astype(BF16)

    my_half = bp.at[:, pl.ds(pl.multiple_of(c * HALF, 128), HALF)]
    other_half = bp.at[:, pl.ds(pl.multiple_of((1 - c) * HALF, 128), HALF)]
    send_bx = remote(bx, my_half, cs.at[3], cr.at[3], partner)
    send_bx.start()

    for side in range(2):
        s2[side].wait_recv()
        place = (p2 + 1 if side == 0 else p2 + 3) % 4
        offset, rows = (0, CUT) if side == 0 else (CUT, PADDED - CUT)

        def add_relay2(r, place=place, offset=offset):
            here = pl.ds(pl.multiple_of(offset + r, 16), 16)
            total[place, here, :] = (
                total[place, here, :].astype(F32) + relay2[here, :].astype(F32)
            ).astype(BF16)

        add_rows(rows, add_relay2)
        r2[side].start()

    remote(bx, other_half, cs.at[3], cr.at[3], partner).wait_recv()

    @pl.loop(0, D // 128)
    def _(t):
        start, pick = compact_tile(t)
        window = bp[:, pl.ds(pl.multiple_of(start, 128), 384)]
        sc[:, pl.ds(pl.multiple_of(t * 128, 128), 128)] = mm(window, pick).astype(BF16)

    store_branch = pltpu.make_async_copy(sc, branch_hbm, out_sem.at[8])
    store_branch.start()

    for copy in (s2[2], s2[3], r2[0], r2[1]):
        copy.wait_recv()

    def add_second(r):
        here = pl.ds(r, 16)
        summed[here, :] = (
            total[p2, here, :].astype(F32)
            + direct2[0, here, :].astype(F32)
            + direct2[1, here, :].astype(F32)
        ).astype(BF16)

    add_rows(PADDED, add_second)

    y_near = [
        remote(summed, ysum.at[0], ys.at[0], yr.at[0], at(x, y + 1, z, c)),
        remote(summed, ysum.at[1], ys.at[1], yr.at[1], at(x, y - 1, z, c)),
    ]
    y_far = remote(summed, ysum.at[2], ys.at[2], yr.at[2], at(x, y + 2, z, c))

    @pl.when(c != yl)
    def _():
        y_near[0].start()
        y_near[1].start()

    @pl.when(c == yl)
    def _():
        y_far.start()

    def backward(slot):
        owner = meta[2, slot]
        for h in range(HEADS):
            cols = slice(h * HEAD, (h + 1) * HEAD)
            kcols = slice(WIDTH + h * HEAD, WIDTH + (h + 1) * HEAD)
            vcols = slice(2 * WIDTH + h * HEAD, 2 * WIDTH + (h + 1) * HEAD)
            q, k, v = qkv[slot, :, cols], qkv[slot, :, kcols], qkv[slot, :, vcols]
            soft = soft_keep[owner, h]
            go = back_recv[owner, :, cols]
            out = att_send[owner, :, cols]
            delta = jnp.sum(go.astype(F32) * out.astype(F32), axis=-1, keepdims=True)
            gs = (soft * (mm(go, v, NT) - delta)).astype(BF16)
            qkv[slot, :, cols] = (mm(gs, k) * INV_SCALE).astype(BF16)
            qkv[slot, :, kcols] = (mm(gs, q, TN) * INV_SCALE).astype(BF16)
            qkv[slot, :, vcols] = mm(soft.astype(BF16), go, TN).astype(BF16)

    def store_slot(slot):
        return pltpu.make_async_copy(qkv.at[slot], qkv_grad_hbm.at[slot], out_sem.at[slot])

    for i in range(7):
        source = (d + 7 - i) % 8
        remote(back_send.at[source], back_recv.at[source], b2s.at[i], b2r.at[i], partner).wait_recv()

    @pl.loop(0, 4)
    def _(slot):
        backward(slot)
        store_slot(slot).start()

    keeper = x // 2
    f_block = x % 2
    f_copies = [
        remote(mixed, final.at[f_block], fs.at[n], fr.at[f_block], at(x + n, y, z, keeper))
        for n in range(4)
    ]

    @pl.when(c == yl)
    def _():
        for copy in (*y_near, y_far):
            copy.wait_recv()

        def add_y(r):
            here = pl.ds(r, 16)
            mixed[here, :] = (
                summed[here, :].astype(F32)
                + ysum[0, here, :].astype(F32)
                + ysum[1, here, :].astype(F32)
                + ysum[2, here, :].astype(F32)
            ).astype(BF16)

        add_rows(PADDED, add_y)
        for n in range(1, 4):
            f_copies[n].start()

        @pl.when(keeper != c)
        def _():
            f_copies[0].start()

    @pl.loop(4, IMGS)
    def _(slot):
        backward(slot)
        store_slot(slot).start()

    mine = (c == yl) & (keeper == c)
    for n in range(2):
        @pl.when(mine & (f_block == n))
        def _():
            final[n] = mixed[...]

        @pl.when(jnp.logical_not(mine & (f_block == n)))
        def _():
            remote(mixed, final.at[n], fs.at[0], fr.at[n], partner).wait_recv()

    @pl.loop(0, SHARD // 16)
    def _(r):
        here = pl.ds(pl.multiple_of(r * 16, 16), 16)
        wout[here, :BLOCK] = final[0, here, :].astype(F32)
        wout[here, SECOND:] = final[1, here, :].astype(F32)

    tail = SHARD - SHARD % 16
    wout[tail:, :BLOCK] = final[0, tail:, :].astype(F32)[: SHARD - tail]
    wout[tail:, SECOND:] = final[1, tail:, :].astype(F32)[: SHARD - tail]

    store_w = pltpu.make_async_copy(wout, weight_grad_hbm, out_sem.at[9])
    store_w.start()

    w_y.wait_send()

    @pl.when(c != yl)
    def _():
        w_c.wait_send()
        y_near[0].wait_send()
        y_near[1].wait_send()

    @pl.when(c == yl)
    def _():
        y_far.wait_send()
        for n in range(1, 4):
            f_copies[n].wait_send()

        @pl.when(keeper != c)
        def _():
            f_copies[0].wait_send()

    for i in range(7):
        att_copy(i).wait_send()
        back_copy(i).wait_send()
    for copy in (*w1, *w2, send_sx, send_aa, send_ga, send_bx, *s1, *r1, *s2, *r2):
        copy.wait_send()
    for slot in range(IMGS):
        store_slot(slot).wait()
    store_branch.wait()
    store_w.wait()


def per_device(
    qkv_rows, proj_weight, layer_scale, out_grad, patch_counts, loader_plan, row_offsets
):
    dp_index = lax.axis_index("dp")
    column = lax.axis_index("fsdp")
    col_plan = lax.dynamic_index_in_dim(loader_plan, column, 1, keepdims=False)
    col_counts = lax.dynamic_index_in_dim(patch_counts, column, 1, keepdims=False)
    my_plan = lax.dynamic_index_in_dim(col_plan, dp_index, 0, keepdims=False)
    my_counts = lax.dynamic_index_in_dim(col_counts, dp_index, 0, keepdims=False)
    my_offsets = row_offsets[dp_index, column]
    ids = jnp.arange(IMGS, dtype=jnp.int32)
    slot_pos = jnp.arange(MAXP, dtype=jnp.int32)
    slot_of_owner = (col_plan == dp_index).astype(jnp.int32)
    meta = jnp.stack(
        [
            jnp.sum(slot_of_owner * ids[None, :], axis=1),
            jnp.sum(slot_of_owner * col_counts, axis=1),
            jnp.sum(slot_of_owner * ids[:, None], axis=0),
        ]
    )
    image_of_loader = my_plan[None, :] == ids[:, None]
    offset_from = jnp.sum(jnp.where(image_of_loader, my_offsets[None, :], 0), axis=1)
    count_from = jnp.sum(jnp.where(image_of_loader, my_counts[None, :], 0), axis=1)
    source = jnp.where(
        slot_pos[None, :] < count_from[:, None], offset_from[:, None] + slot_pos[None, :], -1
    )
    scale_pad = jnp.pad(layer_scale.reshape(16, SHARD), ((0, 0), (0, PADDED - SHARD)))

    vmem = pl.BlockSpec(memory_space=pltpu.VMEM)
    hbm = pl.BlockSpec(memory_space=pl.ANY)
    dma = pltpu.SemaphoreType.DMA
    rows = (PADDED, BLOCK)
    branch, grads, weight_grad = pl.pallas_call(
        fused,
        out_shape=(
            jax.ShapeDtypeStruct((OWN, D), BF16),
            jax.ShapeDtypeStruct((IMGS, MAXP, 3 * WIDTH), BF16),
            jax.ShapeDtypeStruct((SHARD, WIDTH), F32),
        ),
        in_specs=[pl.BlockSpec(memory_space=pltpu.SMEM), hbm, hbm, hbm, vmem, vmem, vmem, vmem],
        out_specs=(hbm, hbm, hbm),
        scratch_shapes=[
            pltpu.VMEM((SHARD, WIDTH), BF16),
            pltpu.VMEM((PADDED, WIDTH), BF16),
            pltpu.VMEM((HALF, WIDTH), BF16),
            pltpu.VMEM((IMGS, MAXP, 3 * WIDTH), BF16),
            pltpu.VMEM((OWN, D), BF16),
            pltpu.VMEM((2 * OWN, HALF), BF16),
            pltpu.VMEM((OWN, HALF), BF16),
            pltpu.VMEM((IMGS, MAXP, WIDTH), BF16),
            pltpu.VMEM((IMGS, MAXP, WIDTH), BF16),
            pltpu.VMEM((2 * OWN, WIDTH), BF16),
            pltpu.VMEM((IMGS, HEADS, MAXP, MAXP), F32),
            pltpu.VMEM((2, HALF, BLOCK), BF16),
            pltpu.VMEM((2, 2, *rows), BF16),
            pltpu.VMEM((2, 4, *rows), BF16),
            pltpu.VMEM((4, *rows), BF16),
            pltpu.VMEM(rows, BF16),
            pltpu.VMEM((2, *rows), BF16),
            pltpu.VMEM(rows, BF16),
            pltpu.VMEM((3, *rows), BF16),
            pltpu.VMEM(rows, BF16),
            pltpu.VMEM((2, *rows), BF16),
            pltpu.VMEM((SHARD, WIDTH), F32),
            pltpu.VMEM((OWN, WIDTH), F32),
            pltpu.VMEM((OWN, WIDTH), F32),
            pltpu.VMEM((OWN, WIDTH), F32),
            pltpu.VMEM((IMGS, MAXP, WIDTH), BF16),
            pltpu.VMEM((IMGS, MAXP, WIDTH), BF16),
            pltpu.VMEM((OWN, 2 * HALF), BF16),
            pltpu.VMEM((OWN, HALF), BF16),
            dma((3,)),
            dma((2,)), dma((2,)),
            dma((6,)), dma((6,)),
            dma((7,)), dma((7,)),
            dma((4,)), dma((4,)),
            dma((12,)), dma((12,)),
            dma((6,)), dma((6,)),
            dma((3,)), dma((3,)),
            dma((4,)), dma((2,)),
            dma((7,)), dma((7,)),
            dma((10,)),
        ],
        compiler_params=pltpu.CompilerParams(
            collective_id=0, has_side_effects=True, vmem_limit_bytes=62 << 20
        ),
        cost_estimate=pl.CostEstimate(
            flops=13_000_000_000, bytes_accessed=20_000_000, transcendentals=500_000
        ),
        name="attention_sublayer",
    )(
        meta,
        proj_weight,
        qkv_rows[0, 0],
        out_grad[0, 0],
        layer_scale[None, :],
        scale_pad.reshape(1, 2 * HALF),
        source.reshape(1, IMGS * MAXP),
        source.reshape(IMGS * MAXP, 1),
    )
    return (branch[None, None], grads[None, None], weight_grad)


def solution(mesh):
    in_specs = (
        P("dp", "fsdp", None, None, None),
        P("fsdp", None),
        P(),
        P("dp", "fsdp", None, None),
        P(),
        P(),
        P(),
    )
    out_specs = (P("dp", "fsdp", None, None), P("dp", "fsdp", None, None, None), P("fsdp", None))
    return jax.shard_map(
        per_device, mesh=mesh, in_specs=in_specs, out_specs=out_specs, check_vma=False
    )
```

```python
import math

import jax
import jax.numpy as jnp
from jax import lax
from jax.experimental import pallas as pl
from jax.experimental.pallas import tpu as pltpu
from jax.sharding import PartitionSpec as P

HEADS = 13
HEAD = 128
WIDTH = HEADS * HEAD
D = 3200
IMGS = 8
MAXP = 64
OWN = 320
SHARD = 200
PADDED = 208
HALF = 8 * PADDED
BLOCK = 896
SECOND = WIDTH - BLOCK
CUT = 96
MASKED = -1e30
TURNS = 0o06725341
MESH = pl.DeviceIdType.MESH
INV_SCALE = 1.0 / math.sqrt(HEAD)
F32 = jnp.float32
BF16 = jnp.bfloat16

NN = (((1,), (0,)), ((), ()))
NT = (((1,), (1,)), ((), ()))
TN = (((0,), (0,)), ((), ()))


def mm(a, b, dims=NN):
    return lax.dot_general(a, b, dims, preferred_element_type=F32)


def two_heads(rows):
    none = jnp.zeros((MAXP, HEAD), BF16)
    upper = jnp.concatenate([rows[:, :HEAD], none], axis=1)
    lower = jnp.concatenate([none, rows[:, HEAD:]], axis=1)
    return jnp.concatenate([upper, lower], axis=0)


def stacked(rows):
    return two_heads(rows) if rows.shape[1] > HEAD else rows


def side_by_side(product):
    if product.shape[0] == MAXP:
        return product
    return jnp.concatenate([product[:MAXP, :HEAD], product[MAXP:, HEAD:]], axis=1)


def unit_columns(unit):
    return slice(2 * unit * HEAD, min(2 * unit + 2, HEADS) * HEAD)


def by_columns(body):
    @pl.loop(0, WIDTH // 256)
    def _(n):
        body(pl.multiple_of(n * 256, 128), 256)

    body(WIDTH - WIDTH % 256, WIDTH % 256)


def spread_tile(tile):
    first = tile * 128
    group = first // PADDED
    inside = first % PADDED
    start = lax.min((group * SHARD + lax.min(inside, SHARD)) // 128, D // 128 - 2)
    place = first + lax.broadcasted_iota(jnp.int32, (256, 128), 1)
    source = start * 128 + lax.broadcasted_iota(jnp.int32, (256, 128), 0)
    groups = group + (place >= (group + 1) * PADDED).astype(jnp.int32)
    local = place - groups * PADDED
    hit = (source == groups * SHARD + local) & (local < SHARD)
    return start * 128, jnp.where(hit, 1.0, 0.0).astype(BF16)


def compact_tile(tile):
    first = tile * 128
    group = first // SHARD
    start = lax.min((first + group * (PADDED - SHARD)) // 128, 2 * HALF // 128 - 3)
    place = first + lax.broadcasted_iota(jnp.int32, (384, 128), 1)
    source = start * 128 + lax.broadcasted_iota(jnp.int32, (384, 128), 0)
    groups = group + (place >= (group + 1) * SHARD).astype(jnp.int32)
    hit = source == place + groups * (PADDED - SHARD)
    return start * 128, jnp.where(hit, 1.0, 0.0).astype(BF16)


def fused(
    tables, shard_hbm, qkv_hbm, grad_hbm, scale,
    branch_hbm, qkv_grad_hbm, final_hbm,
    meta, wv, wp, wh, qkv, sc, scale_parts, scale_pad, sp, sx, att_send, att_recv, aa, soft_keep,
    gh, relay, direct, total, relay2, direct2, summed, ysum, mixed, final,
    ga_own, ga_send, ga_recv, back_send, back_recv, bx,
    in_sem, w0s, w0r, w1s, w1r, a2s, a2r, cs, cr, g1s, g1r, g2s, g2r, ys, yr, fs, fr, b2s, b2r, out_sem,
):
    d = lax.axis_index("dp")
    f = lax.axis_index("fsdp")
    c = f % 2
    z = (f // 2) % 4
    yl = f // 8
    x = d // 2
    y = (d % 2) * 2 + yl

    def at(px, py, pz, pc):
        px, py, pz = (px + 4) % 4, (py + 4) % 4, (pz + 4) % 4
        return (px * 2 + py // 2, ((py % 2) * 4 + pz) * 2 + pc)

    def remote(src, dst, send, recv, dev):
        return pltpu.make_async_remote_copy(
            src_ref=src, dst_ref=dst, send_sem=send, recv_sem=recv, device_id=dev, device_id_type=MESH
        )

    partner = at(x, y, z, 1 - c)

    load_w = pltpu.make_async_copy(shard_hbm, wv, in_sem.at[0])
    load_q = pltpu.make_async_copy(qkv_hbm, qkv, in_sem.at[1])
    load_g = pltpu.make_async_copy(grad_hbm, sc, in_sem.at[2])
    load_w.start()
    load_q.start()
    load_g.start()

    barrier = pltpu.get_barrier_semaphore()
    peers = []
    for step in range(1, 8):
        other = (d + step) % 8
        peers += [(other, f), (other, f + 1 - 2 * c)]
    peers += [partner, at(x, y, z + 1, c), at(x, y, z - 1, c)]
    for sign in (1, -1):
        peers += [at(x, y + sign, z, 0), at(x, y + sign, z, 1)]
    for peer in peers:
        pl.semaphore_signal(barrier, inc=1, device_id=peer, device_id_type=MESH)
    owner_of = [(d + 8 - tables[0, 0, k]) % 8 for k in range(IMGS)]
    for k in range(IMGS):
        meta[2, k] = owner_of[k]
    image_offset, image_count = [], []
    for e in range(8):
        slot, image = 0, 0
        for k in range(1, IMGS):
            slot = jnp.where(owner_of[k] == e, k, slot)
            image = jnp.where(tables[0, d, k] == e, k, image)
        meta[0, e] = slot
        meta[1, e] = tables[1, e, slot]
        image_offset.append(tables[2, d, image])
        image_count.append(tables[1, d, image])
    load_w.wait()
    wp[0:192, :] = wv[0:192, :]
    wp[192:208, :] = jnp.concatenate(
        [wv[192:200, :].astype(F32), jnp.zeros((8, WIDTH), F32)], axis=0
    ).astype(BF16)
    pl.semaphore_wait(barrier, len(peers))

    def w_rows(pz, k):
        return wh.at[pl.ds(pl.multiple_of((((pz + 4) % 4) * 2 + k) * PADDED, 16), PADDED), :]

    w_y = remote(wp, w_rows(z, c), w0s.at[0], w0r.at[c], at(x, y + 1 - 2 * c, z, yl))
    w_c = remote(wp, w_rows(z, c), w0s.at[1], w0r.at[c], partner)
    w_l = pltpu.make_async_copy(wp, w_rows(z, c), w0s.at[1])
    w_y.start()

    @pl.when(c == yl)
    def _():
        w_l.start()

    @pl.when(c != yl)
    def _():
        w_c.start()

    load_q.wait()

    def partner_at(i, sign=1):
        n = TURNS // 8**i % 8 if isinstance(i, int) else lax.div(TURNS, lax.shift_left(1, 3 * i)) % 8
        return ((x + sign * (n % 4) + 4) % 4) * 2 + (d + n // 4) % 2

    def att_copy(i):
        owner = partner_at(i)
        return remote(att_send.at[owner], att_recv.at[d], a2s.at[i], a2r.at[i], (owner, f))

    @pl.loop(0, IMGS)
    def _(i):
        owner = partner_at(i)
        slot = meta[0, owner]
        count = meta[1, owner]
        for units in ((0, 1, 2, 3), (4, 5, 6)):
            scores = []
            for u in units:
                cols = unit_columns(u)
                q = qkv[slot, :, cols]
                k = qkv[slot, :, WIDTH + cols.start : WIDTH + cols.stop]
                scores.append(mm(k, stacked(q), NT) * INV_SCALE)
            softs = []
            for u, s in zip(units, scores):
                s = jnp.where(lax.broadcasted_iota(jnp.int32, s.shape, 0) < count, s, MASKED)
                e = jnp.exp(s - jnp.max(s, axis=0, keepdims=True))
                soft = e * (1.0 / jnp.sum(e, axis=0, keepdims=True))
                soft_keep[owner, u, :, : s.shape[1]] = soft
                softs.append(soft.astype(BF16))
            for u, soft in zip(units, softs):
                cols = unit_columns(u)
                v = qkv[slot, :, 2 * WIDTH + cols.start : 2 * WIDTH + cols.stop]
                att_send[owner, :, cols] = side_by_side(mm(soft, v, TN)).astype(BF16)

        @pl.when(i < 7)
        def _():
            att_copy(i).start()

    att_recv[d] = att_send[d]

    for k in range(2):
        @pl.when((c != yl) | (c != k))
        def _():
            remote(wp, w_rows(z, k), w0s.at[0], w0r.at[k], partner).wait_recv()

    @pl.when(c == yl)
    def _():
        w_l.wait()

    up, down = at(x, y, z + 1, c), at(x, y, z - 1, c)
    w1 = [
        remote(w_rows(z, 0), w_rows(z, 0), w1s.at[0], w1r.at[0], up),
        remote(w_rows(z, 1), w_rows(z, 1), w1s.at[1], w1r.at[1], down),
        remote(w_rows(z, 1), w_rows(z, 1), w1s.at[2], w1r.at[2], up),
        remote(w_rows(z, 0), w_rows(z, 0), w1s.at[3], w1r.at[3], down),
    ]
    for copy in w1:
        copy.start()
    w2 = [
        remote(w_rows(z - 1, 0), w_rows(z - 1, 0), w1s.at[4], w1r.at[4], up),
        remote(w_rows(z + 1, 1), w_rows(z + 1, 1), w1s.at[5], w1r.at[5], down),
    ]

    load_g.wait()

    scale_row = scale[...].reshape(1, D)

    @pl.loop(0, OWN // 16)
    def _(r):
        rows = pl.ds(pl.multiple_of(r * 16, 16), 16)
        sc[rows, :] = (sc[rows, :].astype(F32) * scale_row).astype(BF16)

    high_part = scale_row.astype(BF16).astype(F32)
    mid_part = (scale_row - high_part).astype(BF16).astype(F32)
    low_part = scale_row - high_part - mid_part
    part = lax.broadcasted_iota(jnp.int32, (16, D), 0)
    scale_parts[...] = jnp.where(
        part == 0, high_part, jnp.where(part == 1, mid_part, jnp.where(part == 2, low_part, 0.0))
    ).astype(BF16)

    own_rows = pl.ds(pl.multiple_of(c * OWN, 16), OWN)
    other_rows = pl.ds(pl.multiple_of((1 - c) * OWN, 16), OWN)

    @pl.loop(0, HALF // 128, unroll=True)
    def _(t):
        start, pick = spread_tile((1 - c) * (HALF // 128) + t)
        window = sc[:, pl.ds(pl.multiple_of(start, 128), 256)]
        sx[:, pl.ds(pl.multiple_of(t * 128, 128), 128)] = mm(window, pick).astype(BF16)

    send_sx = remote(sx, sp.at[own_rows, :], cs.at[0], cr.at[0], partner)
    send_sx.start()

    @pl.loop(0, HALF // 128, unroll=True)
    def _(t):
        start, pick = spread_tile(c * (HALF // 128) + t)
        window = sc[:, pl.ds(pl.multiple_of(start, 128), 256)]
        there = pl.ds(pl.multiple_of(t * 128, 128), 128)
        sp[own_rows, there] = mm(window, pick).astype(BF16)
        parts = mm(scale_parts[:, pl.ds(pl.multiple_of(start, 128), 256)], pick)
        scale_pad[:, there] = jnp.sum(parts, axis=0, keepdims=True)

    w1[0].wait_recv()
    w2[0].start()
    w1[1].wait_recv()
    w2[1].start()

    for i in range(7):
        source = partner_at(i, -1)
        remote(att_send.at[source], att_recv.at[source], a2s.at[i], a2r.at[i], partner).wait_recv()
    lane = lax.broadcasted_iota(jnp.int32, (1, IMGS * MAXP), 1)
    source_row = jnp.full((1, IMGS * MAXP), -1, jnp.int32)
    for n in range(8):
        inside = lane - n * MAXP
        source_row = jnp.where(
            (inside >= 0) & (inside < image_count[n]), inside + image_offset[n], source_row
        )
    pack = jnp.where(
        lax.broadcasted_iota(jnp.int32, (OWN, IMGS * MAXP), 0) == source_row, 1.0, 0.0
    ).astype(BF16)

    def pack_columns(start, size):
        got = att_recv[:, :, pl.ds(start, size)].reshape(IMGS * MAXP, size)
        aa[own_rows, pl.ds(start, size)] = mm(pack, got).astype(BF16)

    by_columns(pack_columns)
    send_aa = remote(aa.at[own_rows, :], aa.at[own_rows, :], cs.at[1], cr.at[1], partner)
    send_aa.start()
    remote(sx, sp.at[other_rows, :], cs.at[0], cr.at[0], partner).wait_recv()
    remote(aa.at[other_rows, :], aa.at[other_rows, :], cs.at[1], cr.at[1], partner).wait_recv()

    def block(first, second):
        first, second = (first + 4) % 4, (second + 4) % 4
        return first % 2, pl.ds(pl.multiple_of((second * 2 + first // 2) * PADDED, 16), PADDED)

    p1 = y * (1 - c) + x * c
    p2 = z
    right1, left1 = at(x + c, y + 1 - c, z, c), at(x - c, y - 1 + c, z, c)
    right2, left2 = up, down

    def g1(first, j, dst, sem, dev):
        h, rows = block(first, j)
        return remote(gh.at[h, rows, :], dst, g1s.at[sem], g1r.at[sem], dev)

    s1 = [g1(p1 + 2, j, relay.at[0, j], j, right1) for j in (0, 1)]
    s1 += [g1(p1 + 2, j, relay.at[1, j - 2], j, left1) for j in (2, 3)]
    s1 += [g1(p1 + 1, j, direct.at[0, j], 4 + j, right1) for j in (2, 3)]
    s1 += [g1(p1 - 1, j, direct.at[1, j], 8 + j, left1) for j in (0, 1)]

    def weight_columns(h):
        cols = pl.ds(pl.multiple_of(h * SECOND, 128), BLOCK)

        @pl.loop(0, HALF // 128)
        def _(t):
            rows = pl.ds(pl.multiple_of(t * 128, 128), 128)
            gh[h, rows, :] = mm(sp[:, rows], aa[:, cols], TN).astype(BF16)

    weight_columns(p1 % 2)
    for copy in (s1[0], s1[2], s1[1], s1[3]):
        copy.start()
    weight_columns(1 - p1 % 2)
    for copy in (s1[4], s1[6], s1[5], s1[7]):
        copy.start()
    r1 = [g1(p1 + 1, j, direct.at[0, j], 4 + j, right1) for j in (0, 1)]
    r1 += [g1(p1 - 1, j, direct.at[1, j], 8 + j, left1) for j in (2, 3)]

    def add_rows(rows, body):
        @pl.loop(0, rows // 16)
        def _(r):
            body(pl.multiple_of(r * 16, 16))

    for n, j in enumerate((0, 2, 1, 3)):
        side, place = (0, p1 + 1) if j < 2 else (1, p1 - 1)
        s1[j].wait_recv()
        h, rows = block(place, j)
        base = rows.start

        def add_relay(r, h=h, base=base, side=side, j=j):
            here = pl.ds(pl.multiple_of(base + r, 16), 16)
            gh[h, here, :] = (
                gh[h, here, :].astype(F32) + relay[side, j % 2, pl.ds(r, 16), :].astype(F32)
            ).astype(BF16)

        add_rows(PADDED, add_relay)
        r1[j].start()

    w1[2].wait_recv()
    w1[3].wait_recv()
    w2[0].wait_recv()
    w2[1].wait_recv()

    def grad_columns(start, size):
        cols = pl.ds(start, size)
        ga_send[:, cols] = mm(sp[other_rows, :], wh[:, cols])
        ga_own[:, cols] = mm(sp[own_rows, :], wh[:, cols])

    by_columns(grad_columns)
    send_ga = remote(ga_send, ga_recv, cs.at[2], cr.at[2], partner)
    send_ga.start()
    send_ga.wait_recv()
    unpack = []
    for n in range(8):
        inside = lax.broadcasted_iota(jnp.int32, (MAXP, OWN), 0)
        column = lax.broadcasted_iota(jnp.int32, (MAXP, OWN), 1)
        hit = (inside < image_count[n]) & (column == inside + image_offset[n])
        unpack.append(jnp.where(hit, 1.0, 0.0).astype(BF16))
    unpack = jnp.concatenate(unpack, axis=0)

    def unpack_columns(start, size):
        cols = pl.ds(start, size)
        grad = (ga_own[:, cols] + ga_recv[:, cols]).astype(BF16)
        back_send[:, :, cols] = mm(unpack, grad).astype(BF16).reshape(IMGS, MAXP, size)

    by_columns(unpack_columns)

    def back_copy(i):
        loader = partner_at(i)
        return remote(back_send.at[loader], back_recv.at[d], b2s.at[i], b2r.at[i], (loader, f))

    for i in range(7):
        back_copy(i).start()
    back_recv[d] = back_send[d]

    for j in range(4):
        (s1[4 + j - 2] if j >= 2 else r1[j]).wait_recv()
        (s1[6 + j] if j < 2 else r1[j]).wait_recv()
        h, rows = block(p1, j)
        base = rows.start

        def add_first(r, h=h, base=base, j=j):
            here = pl.ds(r, 16)
            total[j, here, :] = (
                gh[h, pl.ds(pl.multiple_of(base + r, 16), 16), :].astype(F32)
                + direct[0, j, here, :].astype(F32)
                + direct[1, j, here, :].astype(F32)
            ).astype(BF16)

        add_rows(PADDED, add_first)

    low, high = pl.ds(0, CUT), pl.ds(CUT, PADDED - CUT)

    def g2(place, rows, dst, sem, dev):
        return remote(total.at[(place + 4) % 4, rows, :], dst, g2s.at[sem], g2r.at[sem], dev)

    s2 = [
        g2(p2 + 2, low, relay2.at[low, :], 0, right2),
        g2(p2 + 2, high, relay2.at[high, :], 1, left2),
        g2(p2 + 1, high, direct2.at[0, high, :], 2, right2),
        g2(p2 - 1, low, direct2.at[1, low, :], 3, left2),
    ]
    r2 = [
        g2(p2 + 1, low, direct2.at[0, low, :], 4, right2),
        g2(p2 - 1, high, direct2.at[1, high, :], 5, left2),
    ]
    for copy in s2:
        copy.start()

    def project_rows(start, size):
        cols = pl.ds(start, size)
        bx[:, cols] = (scale_pad[:, cols] * mm(aa[...], wh[cols, :], NT)).astype(BF16)

    by_columns(project_rows)
    my_half = branch_hbm.at[:, pl.ds(pl.multiple_of(c * HALF, 128), HALF)]
    other_half = branch_hbm.at[:, pl.ds(pl.multiple_of((1 - c) * HALF, 128), HALF)]
    send_bx = remote(bx.at[other_rows, :], my_half, cs.at[3], cr.at[3], partner)
    send_bx.start()
    store_branch = pltpu.make_async_copy(bx.at[own_rows, :], my_half, out_sem.at[8])
    store_branch.start()

    for side in range(2):
        s2[side].wait_recv()
        place = (p2 + 1 if side == 0 else p2 + 3) % 4
        offset, rows = (0, CUT) if side == 0 else (CUT, PADDED - CUT)

        def add_relay2(r, place=place, offset=offset):
            here = pl.ds(pl.multiple_of(offset + r, 16), 16)
            total[place, here, :] = (
                total[place, here, :].astype(F32) + relay2[here, :].astype(F32)
            ).astype(BF16)

        add_rows(rows, add_relay2)
        r2[side].start()

    for copy in (s2[2], s2[3], r2[0], r2[1]):
        copy.wait_recv()

    def add_second(r):
        here = pl.ds(r, 16)
        summed[here, :] = (
            total[p2, here, :].astype(F32)
            + direct2[0, here, :].astype(F32)
            + direct2[1, here, :].astype(F32)
        ).astype(BF16)

    add_rows(PADDED, add_second)

    s3 = [
        remote(summed, ysum.at[n], ys.at[n], yr.at[n], at(x + (1 - c) * m, y + c * m, z, c))
        for n, m in enumerate((1, 3, 2))
    ]
    for copy in s3:
        copy.start()

    def backward(slot):
        owner = meta[2, slot]
        for units in ((0, 1, 2), (3, 4), (5, 6)):
            stages = []
            for u in units:
                cols = unit_columns(u)
                v = qkv[slot, :, 2 * WIDTH + cols.start : 2 * WIDTH + cols.stop]
                go = stacked(back_recv[owner, :, cols])
                soft = soft_keep[owner, u, :, : go.shape[0]]
                stages.append((u, go, soft, mm(v, go, NT)))
            for u, go, soft, grad_soft in stages:
                cols = unit_columns(u)
                kcols = slice(WIDTH + cols.start, WIDTH + cols.stop)
                vcols = slice(2 * WIDTH + cols.start, 2 * WIDTH + cols.stop)
                q, k = stacked(qkv[slot, :, cols]), qkv[slot, :, kcols]
                delta = jnp.sum(soft * grad_soft, axis=0, keepdims=True)
                gs = (soft * (grad_soft - delta)).astype(BF16)
                grad_v = mm(soft.astype(BF16), go)
                grad_k = mm(gs, q) * INV_SCALE
                grad_q = side_by_side(mm(gs, k, TN)) * INV_SCALE
                qkv[slot, :, vcols] = grad_v.astype(BF16)
                qkv[slot, :, kcols] = grad_k.astype(BF16)
                qkv[slot, :, cols] = grad_q.astype(BF16)

    def store_slot(slot):
        return pltpu.make_async_copy(qkv.at[slot], qkv_grad_hbm.at[slot], out_sem.at[slot])

    for copy in s3:
        copy.wait_recv()

    def add_third(r):
        here = pl.ds(r, 16)
        mixed[here, :] = (
            summed[here, :].astype(F32)
            + ysum[0, here, :].astype(F32)
            + ysum[1, here, :].astype(F32)
            + ysum[2, here, :].astype(F32)
        ).astype(BF16)

    add_rows(PADDED, add_third)
    keeper = p1 // 2
    column = p1 % 2
    mine = (c == yl) & (keeper == c)

    def f_copy(n, dev):
        return remote(mixed, final.at[column], fs.at[n], fr.at[column], dev)

    f_y = [f_copy(n, at(x, 2 * n, z, keeper)) for n in range(2)]
    f_x = [f_copy(n, at(x + n, y, z, keeper)) for n in range(4)]

    def for_spread(act):
        for n in range(2):
            @pl.when((c == 0) & jnp.logical_not(mine & (y == 2 * n)))
            def _():
                act(f_y[n])

        @pl.when((c == 1) & (yl == 1))
        def _():
            for n in (1, 3, 2):
                act(f_x[n])

            @pl.when(jnp.logical_not(mine))
            def _():
                act(f_x[0])

    for_spread(lambda copy: copy.start())

    for i in range(7):
        source = partner_at(i, -1)
        remote(back_send.at[source], back_recv.at[source], b2s.at[i], b2r.at[i], partner).wait_recv()

    @pl.loop(0, IMGS)
    def _(slot):
        backward(slot)
        store_slot(slot).start()

    for n in range(2):
        @pl.when(mine & (column == n))
        def _():
            final[n] = mixed[...]

        @pl.when(jnp.logical_not(mine & (column == n)))
        def _():
            remote(mixed, final.at[n], fs.at[0], fr.at[n], partner).wait_recv()

    store_w = pltpu.make_async_copy(final, final_hbm, out_sem.at[9])
    store_w.start()
    send_bx_recv = remote(bx.at[other_rows, :], other_half, cs.at[3], cr.at[3], partner)
    send_bx_recv.wait_recv()

    w_y.wait_send()

    @pl.when(c != yl)
    def _():
        w_c.wait_send()

    for_spread(lambda copy: copy.wait_send())
    for i in range(7):
        att_copy(i).wait_send()
        back_copy(i).wait_send()
    for copy in (*w1, *w2, send_sx, send_aa, send_ga, send_bx, *s1, *r1, *s2, *r2, *s3):
        copy.wait_send()
    for slot in range(IMGS):
        store_slot(slot).wait()
    store_branch.wait()
    store_w.wait()


def finish(
    branch_hbm, grads_hbm, sums_hbm, branch_out, grads_out, weight_out,
    padded, grads, sums, branch, weight, in_sem, out_sem,
):
    load_branch = pltpu.make_async_copy(branch_hbm, padded, in_sem.at[8])
    load_sums = pltpu.make_async_copy(sums_hbm, sums, in_sem.at[9])
    loads = [pltpu.make_async_copy(grads_hbm.at[k], grads.at[k], in_sem.at[k]) for k in range(IMGS)]
    stores = [pltpu.make_async_copy(grads.at[k], grads_out.at[k], out_sem.at[k]) for k in range(IMGS)]
    store_branch = pltpu.make_async_copy(branch, branch_out, out_sem.at[8])
    store_weight = pltpu.make_async_copy(weight, weight_out, out_sem.at[9])
    load_branch.start()
    load_sums.start()
    for load in loads:
        load.start()
    load_sums.wait()
    weight[:, :BLOCK] = sums[0].astype(F32)[:SHARD]
    weight[:, SECOND:] = sums[1].astype(F32)[:SHARD]
    store_weight.start()
    load_branch.wait()
    for k in range(IMGS):
        loads[k].wait()
        stores[k].start()

    @pl.loop(0, D // 128, unroll=5)
    def _(t):
        start, pick = compact_tile(t)
        window = padded[:, pl.ds(pl.multiple_of(start, 128), 384)]
        branch[:, pl.ds(pl.multiple_of(t * 128, 128), 128)] = mm(window, pick).astype(BF16)

    store_branch.start()
    for store in (store_weight, *stores, store_branch):
        store.wait()


def per_device(
    qkv_rows, proj_weight, layer_scale, out_grad, patch_counts, loader_plan, row_offsets
):
    tables = jnp.stack([loader_plan, patch_counts, row_offsets])
    tables = lax.dynamic_index_in_dim(tables, lax.axis_index("fsdp"), 2, keepdims=False)
    vmem = pl.BlockSpec(memory_space=pltpu.VMEM)
    smem = pl.BlockSpec(memory_space=pltpu.SMEM)
    hbm = pl.BlockSpec(memory_space=pl.ANY)
    dma = pltpu.SemaphoreType.DMA
    rows = (PADDED, BLOCK)
    grads_shape = jax.ShapeDtypeStruct((IMGS, MAXP, 3 * WIDTH), BF16)
    padded_branch, grads, sums = pl.pallas_call(
        fused,
        out_shape=(
            jax.ShapeDtypeStruct((OWN, 2 * HALF), BF16),
            grads_shape,
            jax.ShapeDtypeStruct((2, *rows), BF16),
        ),
        in_specs=[smem, hbm, hbm, hbm, vmem],
        out_specs=(hbm, hbm, hbm),
        scratch_shapes=[
            pltpu.SMEM((3, 8), jnp.int32),
            pltpu.VMEM((SHARD, WIDTH), BF16),
            pltpu.VMEM((PADDED, WIDTH), BF16),
            pltpu.VMEM((HALF, WIDTH), BF16),
            pltpu.VMEM((IMGS, MAXP, 3 * WIDTH), BF16),
            pltpu.VMEM((OWN, D), BF16),
            pltpu.VMEM((16, D), BF16),
            pltpu.VMEM((1, HALF), F32),
            pltpu.VMEM((2 * OWN, HALF), BF16),
            pltpu.VMEM((OWN, HALF), BF16),
            pltpu.VMEM((IMGS, MAXP, WIDTH), BF16),
            pltpu.VMEM((IMGS, MAXP, WIDTH), BF16),
            pltpu.VMEM((2 * OWN, WIDTH), BF16),
            pltpu.VMEM((IMGS, (HEADS + 1) // 2, MAXP, 2 * MAXP), F32),
            pltpu.VMEM((2, HALF, BLOCK), BF16),
            pltpu.VMEM((2, 2, *rows), BF16),
            pltpu.VMEM((2, 4, *rows), BF16),
            pltpu.VMEM((4, *rows), BF16),
            pltpu.VMEM(rows, BF16),
            pltpu.VMEM((2, *rows), BF16),
            pltpu.VMEM(rows, BF16),
            pltpu.VMEM((3, *rows), BF16),
            pltpu.VMEM(rows, BF16),
            pltpu.VMEM((2, *rows), BF16),
            pltpu.VMEM((OWN, WIDTH), F32),
            pltpu.VMEM((OWN, WIDTH), F32),
            pltpu.VMEM((OWN, WIDTH), F32),
            pltpu.VMEM((IMGS, MAXP, WIDTH), BF16),
            pltpu.VMEM((IMGS, MAXP, WIDTH), BF16),
            pltpu.VMEM((2 * OWN, HALF), BF16),
            dma((3,)),
            dma((2,)), dma((2,)),
            dma((6,)), dma((6,)),
            dma((7,)), dma((7,)),
            dma((4,)), dma((4,)),
            dma((12,)), dma((12,)),
            dma((6,)), dma((6,)),
            dma((3,)), dma((3,)),
            dma((4,)), dma((2,)),
            dma((7,)), dma((7,)),
            dma((10,)),
        ],
        compiler_params=pltpu.CompilerParams(
            collective_id=0, has_side_effects=True, vmem_limit_bytes=62 << 20
        ),
        cost_estimate=pl.CostEstimate(
            flops=13_000_000_000, bytes_accessed=20_000_000, transcendentals=500_000
        ),
        name="attention_sublayer",
    )(
        tables,
        proj_weight,
        qkv_rows[0, 0],
        out_grad[0, 0],
        layer_scale,
    )
    branch, grads, weight_grad = pl.pallas_call(
        finish,
        out_shape=(
            jax.ShapeDtypeStruct((OWN, D), BF16),
            grads_shape,
            jax.ShapeDtypeStruct((SHARD, WIDTH), F32),
        ),
        in_specs=[hbm, hbm, hbm],
        out_specs=(hbm, hbm, hbm),
        scratch_shapes=[
            pltpu.VMEM((OWN, 2 * HALF), BF16),
            pltpu.VMEM((IMGS, MAXP, 3 * WIDTH), BF16),
            pltpu.VMEM((2, *rows), BF16),
            pltpu.VMEM((OWN, D), BF16),
            pltpu.VMEM((SHARD, WIDTH), F32),
            dma((10,)),
            dma((10,)),
        ],
        compiler_params=pltpu.CompilerParams(vmem_limit_bytes=60 << 20),
        name="finish",
    )(padded_branch, grads, sums)
    return (branch[None, None], grads[None, None], weight_grad)


def solution(mesh):
    in_specs = (
        P("dp", "fsdp", None, None, None),
        P("fsdp", None),
        P(),
        P("dp", "fsdp", None, None),
        P(),
        P(),
        P(),
    )
    out_specs = (P("dp", "fsdp", None, None), P("dp", "fsdp", None, None, None), P("fsdp", None))
    return jax.shard_map(
        per_device, mesh=mesh, in_specs=in_specs, out_specs=out_specs, check_vma=False
    )
```

```python
import math

import jax
import jax.numpy as jnp
from jax import lax
from jax.experimental import pallas as pl
from jax.experimental.pallas import tpu as pltpu
from jax.sharding import PartitionSpec as P

HEADS = 13
HEAD = 128
WIDTH = HEADS * HEAD
D = 3200
IMGS = 8
MAXP = 64
OWN = 320
SHARD = 200
PADDED = 208
HALF = 8 * PADDED
BLOCK = 896
SECOND = WIDTH - BLOCK
PARTS = ((0, BLOCK), (BLOCK, WIDTH))
CUT = 96
PIECE, STRIDE = 64, 48
MASKED = -1e30
TURNS = 0o06725341
MESH = pl.DeviceIdType.MESH
INV_SCALE = 1.0 / math.sqrt(HEAD)
F32 = jnp.float32
BF16 = jnp.bfloat16

NN = (((1,), (0,)), ((), ()))
NT = (((1,), (1,)), ((), ()))
TN = (((0,), (0,)), ((), ()))


def mm(a, b, dims=NN):
    return lax.dot_general(a, b, dims, preferred_element_type=F32)


def two_heads(rows):
    none = jnp.zeros((MAXP, HEAD), BF16)
    upper = jnp.concatenate([rows[:, :HEAD], none], axis=1)
    lower = jnp.concatenate([none, rows[:, HEAD:]], axis=1)
    return jnp.concatenate([upper, lower], axis=0)


def stacked(rows):
    return two_heads(rows) if rows.shape[1] > HEAD else rows


def side_by_side(product):
    if product.shape[0] == MAXP:
        return product
    return jnp.concatenate([product[:MAXP, :HEAD], product[MAXP:, HEAD:]], axis=1)


def unit_columns(unit):
    first = 2 * unit - (unit > 3)
    return slice(first * HEAD, (first + 2 - (unit == 3)) * HEAD)


def by_columns(body, first=0, last=WIDTH):
    whole = (last - first) // 256

    @pl.loop(0, whole)
    def _(n):
        body(pl.multiple_of(first + n * 256, 128), 256)

    if (last - first) % 256:
        body(first + whole * 256, (last - first) % 256)


def spread_tile(tile):
    first = tile * 128
    group = first // PADDED
    inside = first % PADDED
    start = lax.min((group * SHARD + lax.min(inside, SHARD)) // 128, D // 128 - 2)
    place = first + lax.broadcasted_iota(jnp.int32, (256, 128), 1)
    source = start * 128 + lax.broadcasted_iota(jnp.int32, (256, 128), 0)
    groups = group + (place >= (group + 1) * PADDED).astype(jnp.int32)
    local = place - groups * PADDED
    hit = (source == groups * SHARD + local) & (local < SHARD)
    return start * 128, jnp.where(hit, 1.0, 0.0).astype(BF16)


def compact_tile(tile):
    first = tile * 128
    group = first // SHARD
    start = lax.min((first + group * (PADDED - SHARD)) // 128, 2 * HALF // 128 - 3)
    place = first + lax.broadcasted_iota(jnp.int32, (384, 128), 1)
    source = start * 128 + lax.broadcasted_iota(jnp.int32, (384, 128), 0)
    groups = group + (place >= (group + 1) * SHARD).astype(jnp.int32)
    hit = source == place + groups * (PADDED - SHARD)
    return start * 128, jnp.where(hit, 1.0, 0.0).astype(BF16)


def fused(
    tables, shard_hbm, qkv_hbm, grad_hbm, scale,
    branch_hbm, qkv_grad_hbm, final_hbm,
    meta, wv, wp, wh, qkv, sc, scale_parts, scale_pad, sp, sx, att_send, att_recv, aa, soft_keep,
    gh, relay, direct, total, relay2, direct2, summed, ysum, mixed, final,
    ga_own, ga_send, ga_recv, back_send, back_first, back_second, bx, bp,
    in_sem, w0s, w0r, w1s, w1r, w3s, w3r, a2s, a2r, cs, cr, g1s, g1r, g2s, g2r, ys, yr, fs, fr, b2s, b2r, out_sem,
):
    d = lax.axis_index("dp")
    f = lax.axis_index("fsdp")
    c = f % 2
    z = (f // 2) % 4
    yl = f // 8
    x = d // 2
    y = (d % 2) * 2 + yl

    def at(px, py, pz, pc):
        px, py, pz = (px + 4) % 4, (py + 4) % 4, (pz + 4) % 4
        return (px * 2 + py // 2, ((py % 2) * 4 + pz) * 2 + pc)

    def remote(src, dst, send, recv, dev):
        return pltpu.make_async_remote_copy(
            src_ref=src, dst_ref=dst, send_sem=send, recv_sem=recv, device_id=dev, device_id_type=MESH
        )

    partner = at(x, y, z, 1 - c)

    load_w = pltpu.make_async_copy(shard_hbm, wv, in_sem.at[0])
    load_q = pltpu.make_async_copy(qkv_hbm, qkv, in_sem.at[1])
    load_g = pltpu.make_async_copy(grad_hbm, sc, in_sem.at[2])
    load_w.start()
    load_q.start()
    load_g.start()

    barrier = pltpu.get_barrier_semaphore()
    peers = [at(x, y, z + 1, c), at(x, y, z - 1, c), partner]
    for place in range(1, 16):
        for core in range(2):
            peers.append(at(x + place % 4, y + place // 4, z, core))
    for peer in peers:
        pl.semaphore_signal(barrier, inc=1, device_id=peer, device_id_type=MESH)
    owner_of = [(d + 8 - tables[0, 0, k]) % 8 for k in range(IMGS)]
    for k in range(IMGS):
        meta[2, k] = owner_of[k]
    image_offset, image_count = [], []
    for e in range(8):
        slot, image = 0, 0
        for k in range(1, IMGS):
            slot = jnp.where(owner_of[k] == e, k, slot)
            image = jnp.where(tables[0, d, k] == e, k, image)
        meta[0, e] = slot
        meta[1, e] = tables[1, e, slot]
        image_offset.append(tables[2, d, image])
        image_count.append(tables[1, d, image])
    load_w.wait()
    wp[0:192, :] = wv[0:192, :]
    wp[192:208, :] = jnp.concatenate(
        [wv[192:200, :].astype(F32), jnp.zeros((8, WIDTH), F32)], axis=0
    ).astype(BF16)
    pl.semaphore_wait(barrier, len(peers))

    def w_rows(pz, k):
        return wh.at[pl.ds(pl.multiple_of((((pz + 4) % 4) * 2 + k) * PADDED, 16), PADDED), :]

    w_y = remote(wp, w_rows(z, c), w0s.at[0], w0r.at[c], at(x, y + 1 - 2 * c, z, yl))
    w_c = remote(wp, w_rows(z, c), w0s.at[1], w0r.at[c], partner)
    w_l = pltpu.make_async_copy(wp, w_rows(z, c), w0s.at[1])
    w_y.start()

    @pl.when(c == yl)
    def _():
        w_l.start()

    @pl.when(c != yl)
    def _():
        w_c.start()

    load_q.wait()

    def partner_at(i, sign=1):
        n = TURNS // 8**i % 8 if isinstance(i, int) else lax.div(TURNS, lax.shift_left(1, 3 * i)) % 8
        return ((x + sign * (n % 4) + 4) % 4) * 2 + (d + n // 4) % 2

    def att_copy(i):
        owner = partner_at(i)
        return remote(att_send.at[owner], att_recv.at[d], a2s.at[i], a2r.at[i], (owner, f))

    @pl.loop(0, IMGS)
    def _(i):
        owner = partner_at(i)
        slot = meta[0, owner]
        count = meta[1, owner]
        for units in ((0, 1, 2, 3), (4, 5, 6)):
            scores = []
            for u in units:
                cols = unit_columns(u)
                q = qkv[slot, :, cols]
                k = qkv[slot, :, WIDTH + cols.start : WIDTH + cols.stop]
                scores.append(mm(k, stacked(q), NT) * INV_SCALE)
            softs = []
            for u, s in zip(units, scores):
                s = jnp.where(lax.broadcasted_iota(jnp.int32, s.shape, 0) < count, s, MASKED)
                e = jnp.exp(s - jnp.max(s, axis=0, keepdims=True))
                soft = e * (1.0 / jnp.sum(e, axis=0, keepdims=True))
                soft_keep[owner, u, :, : s.shape[1]] = soft
                softs.append(soft.astype(BF16))
            for u, soft in zip(units, softs):
                cols = unit_columns(u)
                v = qkv[slot, :, 2 * WIDTH + cols.start : 2 * WIDTH + cols.stop]
                att_send[owner, :, cols] = side_by_side(mm(soft, v, TN)).astype(BF16)

        @pl.when(i < 7)
        def _():
            att_copy(i).start()

    att_recv[d] = att_send[d]

    for k in range(2):
        @pl.when((c != yl) | (c != k))
        def _():
            remote(wp, w_rows(z, k), w0s.at[0], w0r.at[k], partner).wait_recv()

    @pl.when(c == yl)
    def _():
        w_l.wait()

    up, down = at(x, y, z + 1, c), at(x, y, z - 1, c)
    w1 = [
        remote(w_rows(z, 0), w_rows(z, 0), w1s.at[0], w1r.at[0], up),
        remote(w_rows(z, 1), w_rows(z, 1), w1s.at[1], w1r.at[1], down),
        remote(w_rows(z, 1), w_rows(z, 1), w1s.at[2], w1r.at[2], up),
        remote(w_rows(z, 0), w_rows(z, 0), w1s.at[3], w1r.at[3], down),
    ]

    @pl.when(c == yl)
    def _():
        for copy in w1:
            copy.start()

    w2 = [
        remote(w_rows(z - 1, 0), w_rows(z - 1, 0), w1s.at[4], w1r.at[4], up),
        remote(w_rows(z + 1, 1), w_rows(z + 1, 1), w1s.at[5], w1r.at[5], down),
    ]

    load_g.wait()

    scale_row = scale[...].reshape(1, D)

    @pl.loop(0, OWN // 16)
    def _(r):
        rows = pl.ds(pl.multiple_of(r * 16, 16), 16)
        sc[rows, :] = (sc[rows, :].astype(F32) * scale_row).astype(BF16)

    high_part = scale_row.astype(BF16).astype(F32)
    mid_part = (scale_row - high_part).astype(BF16).astype(F32)
    low_part = scale_row - high_part - mid_part
    part = lax.broadcasted_iota(jnp.int32, (16, D), 0)
    scale_parts[...] = jnp.where(
        part == 0, high_part, jnp.where(part == 1, mid_part, jnp.where(part == 2, low_part, 0.0))
    ).astype(BF16)

    own_rows = pl.ds(pl.multiple_of(c * OWN, 16), OWN)
    other_rows = pl.ds(pl.multiple_of((1 - c) * OWN, 16), OWN)

    @pl.loop(0, HALF // 128, unroll=True)
    def _(t):
        start, pick = spread_tile((1 - c) * (HALF // 128) + t)
        window = sc[:, pl.ds(pl.multiple_of(start, 128), 256)]
        sx[:, pl.ds(pl.multiple_of(t * 128, 128), 128)] = mm(window, pick).astype(BF16)

    send_sx = remote(sx, sp.at[own_rows, :], cs.at[0], cr.at[0], partner)
    send_sx.start()

    @pl.loop(0, HALF // 128, unroll=True)
    def _(t):
        start, pick = spread_tile(c * (HALF // 128) + t)
        window = sc[:, pl.ds(pl.multiple_of(start, 128), 256)]
        there = pl.ds(pl.multiple_of(t * 128, 128), 128)
        sp[own_rows, there] = mm(window, pick).astype(BF16)
        parts = mm(scale_parts[:, pl.ds(pl.multiple_of(start, 128), 256)], pick)
        scale_pad[:, there] = jnp.sum(parts, axis=0, keepdims=True)

    def w_on(step, k):
        pz = z + (1, -1, 2)[step]
        sem = 2 * step + k
        return remote(
            w_rows(pz, k), w_rows(pz, k), w3s.at[sem], w3r.at[sem], at(x, y + 1 - 2 * k, z, c)
        )

    @pl.when(c == yl)
    def _():
        w1[0].wait_recv()
        w2[0].start()
        w_on(1, 0).start()
        w1[1].wait_recv()
        w2[1].start()
        w_on(0, 1).start()
        w1[2].wait_recv()
        w_on(1, 1).start()
        w1[3].wait_recv()
        w_on(0, 0).start()
        for k in range(2):
            w2[k].wait_recv()
            w_on(2, k).start()

    for i in range(7):
        source = partner_at(i, -1)
        remote(att_send.at[source], att_recv.at[source], a2s.at[i], a2r.at[i], partner).wait_recv()
    lane = lax.broadcasted_iota(jnp.int32, (1, IMGS * MAXP), 1)
    source_row = jnp.full((1, IMGS * MAXP), -1, jnp.int32)
    for n in range(8):
        inside = lane - n * MAXP
        source_row = jnp.where(
            (inside >= 0) & (inside < image_count[n]), inside + image_offset[n], source_row
        )
    pack = jnp.where(
        lax.broadcasted_iota(jnp.int32, (OWN, IMGS * MAXP), 0) == source_row, 1.0, 0.0
    ).astype(BF16)

    def pack_columns(start, size):
        got = att_recv[:, :, pl.ds(start, size)].reshape(IMGS * MAXP, size)
        aa[own_rows, pl.ds(start, size)] = mm(pack, got).astype(BF16)

    by_columns(pack_columns)
    send_aa = remote(aa.at[own_rows, :], aa.at[own_rows, :], cs.at[1], cr.at[1], partner)
    send_aa.start()
    remote(sx, sp.at[other_rows, :], cs.at[0], cr.at[0], partner).wait_recv()
    remote(aa.at[other_rows, :], aa.at[other_rows, :], cs.at[1], cr.at[1], partner).wait_recv()

    def block(first, second):
        first, second = (first + 4) % 4, (second + 4) % 4
        pz = first * (1 - c) + second * c
        kh = second * (1 - c) + first * c
        return kh % 2, pl.ds(pl.multiple_of((pz * 2 + kh // 2) * PADDED, 16), PADDED)

    p1 = z * (1 - c) + x * c
    p2 = y * (1 - c) + z * c
    right1, left1 = at(x + c, y, z + 1 - c, c), at(x - c, y, z - 1 + c, c)
    right2, left2 = at(x, y + 1 - c, z + c, c), at(x, y - 1 + c, z - c, c)

    def g1(first, j, dst, sem, dev):
        h, rows = block(first, j)
        return remote(gh.at[h, rows, :], dst, g1s.at[sem], g1r.at[sem], dev)

    s1 = [g1(p1 + 2, j, relay.at[0, j], j, right1) for j in (0, 1)]
    s1 += [g1(p1 + 2, j, relay.at[1, j - 2], j, left1) for j in (2, 3)]
    s1 += [g1(p1 + 1, j, direct.at[0, j], 4 + j, right1) for j in (2, 3)]
    s1 += [g1(p1 - 1, j, direct.at[1, j], 8 + j, left1) for j in (0, 1)]

    def weight_columns(h):
        cols = pl.ds(pl.multiple_of(h * SECOND, 128), BLOCK)

        @pl.loop(0, HALF // 128)
        def _(t):
            rows = pl.ds(pl.multiple_of(t * 128, 128), 128)
            gh[h, rows, :] = mm(sp[:, rows], aa[:, cols], TN).astype(BF16)

    weight_columns(0)
    weight_columns(1)
    first_sends = [s1[n] for n in (0, 2, 1, 3, 4, 6, 5, 7)]

    for copy in first_sends:
        copy.start()
    r1 = [g1(p1 + 1, j, direct.at[0, j], 4 + j, right1) for j in (0, 1)]
    r1 += [g1(p1 - 1, j, direct.at[1, j], 8 + j, left1) for j in (2, 3)]

    def add_rows(rows, body):
        @pl.loop(0, rows // 16)
        def _(r):
            body(pl.multiple_of(r * 16, 16))

    @pl.when(c != yl)
    def _():
        for step in range(3):
            for k in range(2):
                w_on(step, k).wait_recv()

    def grad_columns(start, size):
        cols = pl.ds(start, size)
        ga_send[:, cols] = mm(sp[other_rows, :], wh[:, cols])
        ga_own[:, cols] = mm(sp[own_rows, :], wh[:, cols])

    send_ga = []
    for n, (first, last) in enumerate(PARTS):
        by_columns(grad_columns, first, last)
        cols = pl.ds(first, last - first)
        send_ga.append(
            remote(ga_send.at[:, cols], ga_recv.at[:, cols], cs.at[2 + n], cr.at[2 + n], partner)
        )
        send_ga[n].start()
    unpack = []
    for n in range(8):
        inside = lax.broadcasted_iota(jnp.int32, (MAXP, OWN), 0)
        column = lax.broadcasted_iota(jnp.int32, (MAXP, OWN), 1)
        hit = (inside < image_count[n]) & (column == inside + image_offset[n])
        unpack.append(jnp.where(hit, 1.0, 0.0).astype(BF16))
    unpack = jnp.concatenate(unpack, axis=0)

    def unpack_columns(start, size):
        cols = pl.ds(start, size)
        grad = (ga_own[:, cols] + ga_recv[:, cols]).astype(BF16)
        back_send[:, :, cols] = mm(unpack, grad).astype(BF16).reshape(IMGS, MAXP, size)

    back_parts = (back_first, back_second)

    def back_copy(i, n):
        loader = partner_at(i)
        cols = pl.ds(PARTS[n][0], PARTS[n][1] - PARTS[n][0])
        return remote(
            back_send.at[loader, :, cols], back_parts[n].at[d],
            b2s.at[7 * n + i], b2r.at[7 * n + i], (loader, f),
        )

    for n, j in enumerate((0, 2, 1, 3)):
        side, place = (0, p1 + 1) if j < 2 else (1, p1 - 1)
        s1[j].wait_recv()
        h, rows = block(place, j)
        base = rows.start

        def add_relay(r, h=h, base=base, side=side, j=j):
            here = pl.ds(pl.multiple_of(base + r, 16), 16)
            gh[h, here, :] = (
                gh[h, here, :].astype(F32) + relay[side, j % 2, pl.ds(r, 16), :].astype(F32)
            ).astype(BF16)

        add_rows(PADDED, add_relay)
        r1[j].start()

    for n in range(2):
        send_ga[n].wait_recv()
        by_columns(unpack_columns, *PARTS[n])
        for i in range(7):
            back_copy(i, n).start()
    for n in range(2):
        back_parts[n][d] = back_send[d, :, PARTS[n][0] : PARTS[n][1]]

    for j in range(4):
        (s1[4 + j - 2] if j >= 2 else r1[j]).wait_recv()
        (s1[6 + j] if j < 2 else r1[j]).wait_recv()
        h, rows = block(p1, j)
        base = rows.start

        def add_first(r, h=h, base=base, j=j):
            here = pl.ds(r, 16)
            total[j, here, :] = (
                gh[h, pl.ds(pl.multiple_of(base + r, 16), 16), :].astype(F32)
                + direct[0, j, here, :].astype(F32)
                + direct[1, j, here, :].astype(F32)
            ).astype(BF16)

        add_rows(PADDED, add_first)

    low, high = pl.ds(0, CUT), pl.ds(CUT, PADDED - CUT)

    def g2(place, rows, dst, sem, dev):
        return remote(total.at[(place + 4) % 4, rows, :], dst, g2s.at[sem], g2r.at[sem], dev)

    s2 = [
        g2(p2 + 2, low, relay2.at[low, :], 0, right2),
        g2(p2 + 2, high, relay2.at[high, :], 1, left2),
        g2(p2 + 1, high, direct2.at[0, high, :], 2, right2),
        g2(p2 - 1, low, direct2.at[1, low, :], 3, left2),
    ]
    r2 = [
        g2(p2 + 1, low, direct2.at[0, low, :], 4, right2),
        g2(p2 - 1, high, direct2.at[1, high, :], 5, left2),
    ]
    for copy in s2:
        copy.start()

    def project_rows(start, size):
        cols = pl.ds(start, size)
        bx[:, cols] = (scale_pad[:, cols] * mm(aa[...], wh[cols, :], NT)).astype(BF16)

    by_columns(project_rows)
    my_half = bp.at[:, pl.ds(pl.multiple_of(c * HALF, 128), HALF)]
    other_half = bp.at[:, pl.ds(pl.multiple_of((1 - c) * HALF, 128), HALF)]
    send_bx = remote(bx.at[other_rows, :], my_half, cs.at[4], cr.at[4], partner)
    send_bx.start()
    keep_bx = pltpu.make_async_copy(bx.at[own_rows, :], my_half, out_sem.at[10])
    keep_bx.start()

    for side in range(2):
        s2[side].wait_recv()
        place = (p2 + 1 if side == 0 else p2 + 3) % 4
        offset, rows = (0, CUT) if side == 0 else (CUT, PADDED - CUT)

        def add_relay2(r, place=place, offset=offset):
            here = pl.ds(pl.multiple_of(offset + r, 16), 16)
            total[place, here, :] = (
                total[place, here, :].astype(F32) + relay2[here, :].astype(F32)
            ).astype(BF16)

        add_rows(rows, add_relay2)
        r2[side].start()

    for copy in (s2[2], s2[3], r2[0], r2[1]):
        copy.wait_recv()

    def add_second(r):
        here = pl.ds(r, 16)
        summed[here, :] = (
            total[p2, here, :].astype(F32)
            + direct2[0, here, :].astype(F32)
            + direct2[1, here, :].astype(F32)
        ).astype(BF16)

    add_rows(PADDED, add_second)

    p3 = x * (1 - c) + y * c

    def piece(place):
        return pl.ds(pl.multiple_of((place + 4) % 4 * STRIDE, 16), PIECE)

    s3 = [
        remote(
            summed.at[piece(p3 + m), :], ysum.at[n], ys.at[n], yr.at[n],
            at(x + (1 - c) * m, y + c * m, z, c),
        )
        for n, m in enumerate((1, 3, 2))
    ]
    for copy in s3:
        copy.start()

    keep_bx.wait()
    remote(bx.at[other_rows, :], other_half, cs.at[4], cr.at[4], partner).wait_recv()

    @pl.loop(0, D // 128, unroll=5)
    def _(t):
        start, pick = compact_tile(t)
        window = bp[:, pl.ds(pl.multiple_of(start, 128), 384)]
        sc[:, pl.ds(pl.multiple_of(t * 128, 128), 128)] = mm(window, pick).astype(BF16)

    store_branch = pltpu.make_async_copy(sc, branch_hbm, out_sem.at[8])
    store_branch.start()

    for copy in s3:
        copy.wait_recv()

    @pl.loop(0, PIECE // 16)
    def _(r):
        here = pl.ds(pl.multiple_of(r * 16, 16), 16)
        there = pl.ds(pl.multiple_of(p3 * STRIDE + r * 16, 16), 16)
        mixed[here, :] = (
            summed[there, :].astype(F32)
            + ysum[0, here, :].astype(F32)
            + ysum[1, here, :].astype(F32)
            + ysum[2, here, :].astype(F32)
        ).astype(BF16)

    kept = y * (1 - c) + x * c
    keeper = kept // 2
    column = kept % 2
    mine = (c == yl) & (keeper == c)

    def for_spread(act):
        for n in (1, 3, 2, 0):
            for m in range(2):
                copy = remote(
                    mixed, final.at[column, p3], fs.at[2 * n + m], fr.at[column * 4 + p3],
                    at(x + n, c + 2 * m, z, keeper),
                )
                if n:
                    act(copy)
                else:
                    @pl.when(jnp.logical_not((y == c + 2 * m) & (keeper == c)))
                    def _():
                        act(copy)

    for_spread(lambda copy: copy.start())

    def backward(slot, groups):
        owner = meta[2, slot]
        for units in groups:
            stages = []
            for u in units:
                cols = unit_columns(u)
                v = qkv[slot, :, 2 * WIDTH + cols.start : 2 * WIDTH + cols.stop]
                skip, got = (0, back_first) if u < 4 else (BLOCK, back_second)
                go = stacked(got[owner, :, cols.start - skip : cols.stop - skip])
                soft = soft_keep[owner, u, :, : go.shape[0]]
                stages.append((u, go, soft, mm(v, go, NT)))
            for u, go, soft, grad_soft in stages:
                cols = unit_columns(u)
                kcols = slice(WIDTH + cols.start, WIDTH + cols.stop)
                vcols = slice(2 * WIDTH + cols.start, 2 * WIDTH + cols.stop)
                q, k = stacked(qkv[slot, :, cols]), qkv[slot, :, kcols]
                delta = jnp.sum(soft * grad_soft, axis=0, keepdims=True)
                gs = (soft * (grad_soft - delta)).astype(BF16)
                grad_v = mm(soft.astype(BF16), go)
                grad_k = mm(gs, q) * INV_SCALE
                grad_q = side_by_side(mm(gs, k, TN)) * INV_SCALE
                qkv[slot, :, vcols] = grad_v.astype(BF16)
                qkv[slot, :, kcols] = grad_k.astype(BF16)
                qkv[slot, :, cols] = grad_q.astype(BF16)

    def store_slot(slot):
        return pltpu.make_async_copy(qkv.at[slot], qkv_grad_hbm.at[slot], out_sem.at[slot])

    def wait_back(n):
        for i in range(7):
            source = partner_at(i, -1)
            cols = pl.ds(PARTS[n][0], PARTS[n][1] - PARTS[n][0])
            remote(
                back_send.at[source, :, cols], back_parts[n].at[source],
                b2s.at[7 * n + i], b2r.at[7 * n + i], partner,
            ).wait_recv()

    wait_back(0)

    @pl.loop(0, IMGS)
    def _(slot):
        backward(slot, ((0, 1), (2, 3)))

    wait_back(1)

    @pl.loop(0, IMGS)
    def _(slot):
        backward(slot, ((4, 5, 6),))
        store_slot(slot).start()

    for n in range(2):
        for q in range(4):
            own = mine & (column == n) & (p3 == q)

            @pl.when(own)
            def _():
                final[n, q] = mixed[...]

            @pl.when(jnp.logical_not(own))
            def _():
                remote(mixed, final.at[n, q], fs.at[0], fr.at[n * 4 + q], partner).wait_recv()

    store_w = pltpu.make_async_copy(final, final_hbm, out_sem.at[9])
    store_w.start()
    w_y.wait_send()

    @pl.when(c != yl)
    def _():
        w_c.wait_send()

    @pl.when(c == yl)
    def _():
        for copy in (*w1, *w2):
            copy.wait_send()
        for step in range(3):
            for k in range(2):
                w_on(step, k).wait_send()

    for_spread(lambda copy: copy.wait_send())
    for i in range(7):
        att_copy(i).wait_send()
        back_copy(i, 0).wait_send()
        back_copy(i, 1).wait_send()
    for copy in (send_sx, send_aa, *send_ga, send_bx, *s1, *r1, *s2, *r2, *s3):
        copy.wait_send()
    for slot in range(IMGS):
        store_slot(slot).wait()
    store_branch.wait()
    store_w.wait()


def finish(
    branch_hbm, grads_hbm, sums_hbm, branch_out, grads_out, weight_out,
    branch, grads, sums, weight, in_sem, out_sem,
):
    load_branch = pltpu.make_async_copy(branch_hbm, branch, in_sem.at[8])
    load_sums = pltpu.make_async_copy(sums_hbm, sums, in_sem.at[9])
    loads = [pltpu.make_async_copy(grads_hbm.at[k], grads.at[k], in_sem.at[k]) for k in range(IMGS)]
    stores = [pltpu.make_async_copy(grads.at[k], grads_out.at[k], out_sem.at[k]) for k in range(IMGS)]
    store_branch = pltpu.make_async_copy(branch, branch_out, out_sem.at[8])
    store_weight = pltpu.make_async_copy(weight, weight_out, out_sem.at[9])
    load_sums.start()
    for load in loads:
        load.start()
    load_branch.start()
    load_sums.wait()
    for q in range(4):
        size = STRIDE if q < 3 else SHARD - 3 * STRIDE
        here = slice(q * STRIDE, q * STRIDE + size)
        weight[here, :BLOCK] = sums[0, q].astype(F32)[:size]
        weight[here, SECOND:] = sums[1, q].astype(F32)[:size]
    store_weight.start()
    for k in range(IMGS):
        loads[k].wait()
        stores[k].start()
    load_branch.wait()
    store_branch.start()
    for store in (store_weight, *stores, store_branch):
        store.wait()


def per_device(
    qkv_rows, proj_weight, layer_scale, out_grad, patch_counts, loader_plan, row_offsets
):
    tables = [jnp.swapaxes(table, 1, 2) for table in (loader_plan, patch_counts, row_offsets)]
    tables = lax.dynamic_index_in_dim(
        jnp.stack(tables), lax.axis_index("fsdp"), 3, keepdims=False
    )
    vmem = pl.BlockSpec(memory_space=pltpu.VMEM)
    smem = pl.BlockSpec(memory_space=pltpu.SMEM)
    hbm = pl.BlockSpec(memory_space=pl.ANY)
    dma = pltpu.SemaphoreType.DMA
    rows = (PADDED, BLOCK)
    grads_shape = jax.ShapeDtypeStruct((IMGS, MAXP, 3 * WIDTH), BF16)
    branch, grads, sums = pl.pallas_call(
        fused,
        out_shape=(
            jax.ShapeDtypeStruct((OWN, D), BF16),
            grads_shape,
            jax.ShapeDtypeStruct((2, 4, PIECE, BLOCK), BF16),
        ),
        in_specs=[smem, hbm, hbm, hbm, vmem],
        out_specs=(hbm, hbm, hbm),
        scratch_shapes=[
            pltpu.SMEM((3, 8), jnp.int32),
            pltpu.VMEM((SHARD, WIDTH), BF16),
            pltpu.VMEM((PADDED, WIDTH), BF16),
            pltpu.VMEM((HALF, WIDTH), BF16),
            pltpu.VMEM((IMGS, MAXP, 3 * WIDTH), BF16),
            pltpu.VMEM((OWN, D), BF16),
            pltpu.VMEM((16, D), BF16),
            pltpu.VMEM((1, HALF), F32),
            pltpu.VMEM((2 * OWN, HALF), BF16),
            pltpu.VMEM((OWN, HALF), BF16),
            pltpu.VMEM((IMGS, MAXP, WIDTH), BF16),
            pltpu.VMEM((IMGS, MAXP, WIDTH), BF16),
            pltpu.VMEM((2 * OWN, WIDTH), BF16),
            pltpu.VMEM((IMGS, (HEADS + 1) // 2, MAXP, 2 * MAXP), F32),
            pltpu.VMEM((2, HALF, BLOCK), BF16),
            pltpu.VMEM((2, 2, *rows), BF16),
            pltpu.VMEM((2, 4, *rows), BF16),
            pltpu.VMEM((4, *rows), BF16),
            pltpu.VMEM(rows, BF16),
            pltpu.VMEM((2, *rows), BF16),
            pltpu.VMEM(rows, BF16),
            pltpu.VMEM((3, PIECE, BLOCK), BF16),
            pltpu.VMEM((PIECE, BLOCK), BF16),
            pltpu.VMEM((2, 4, PIECE, BLOCK), BF16),
            pltpu.VMEM((OWN, WIDTH), F32),
            pltpu.VMEM((OWN, WIDTH), F32),
            pltpu.VMEM((OWN, WIDTH), F32),
            pltpu.VMEM((IMGS, MAXP, WIDTH), BF16),
            pltpu.VMEM((IMGS, MAXP, BLOCK), BF16),
            pltpu.VMEM((IMGS, MAXP, WIDTH - BLOCK), BF16),
            pltpu.VMEM((2 * OWN, HALF), BF16),
            pltpu.VMEM((OWN, 2 * HALF), BF16),
            dma((3,)),
            dma((2,)), dma((2,)),
            dma((6,)), dma((6,)),
            dma((6,)), dma((6,)),
            dma((7,)), dma((7,)),
            dma((5,)), dma((5,)),
            dma((12,)), dma((12,)),
            dma((6,)), dma((6,)),
            dma((3,)), dma((3,)),
            dma((8,)), dma((8,)),
            dma((14,)), dma((14,)),
            dma((11,)),
        ],
        compiler_params=pltpu.CompilerParams(
            collective_id=0, has_side_effects=True, vmem_limit_bytes=62 << 20
        ),
        cost_estimate=pl.CostEstimate(
            flops=13_000_000_000, bytes_accessed=20_000_000, transcendentals=500_000
        ),
        name="attention_sublayer",
    )(
        tables,
        proj_weight,
        qkv_rows[0, 0],
        out_grad[0, 0],
        layer_scale,
    )
    branch_rows, grads, weight_grad = pl.pallas_call(
        finish,
        out_shape=(
            jax.ShapeDtypeStruct((OWN, D), BF16),
            grads_shape,
            jax.ShapeDtypeStruct((SHARD, WIDTH), F32),
        ),
        in_specs=[hbm, hbm, hbm],
        out_specs=(hbm, hbm, hbm),
        scratch_shapes=[
            pltpu.VMEM((OWN, D), BF16),
            pltpu.VMEM((IMGS, MAXP, 3 * WIDTH), BF16),
            pltpu.VMEM((2, 4, PIECE, BLOCK), BF16),
            pltpu.VMEM((SHARD, WIDTH), F32),
            dma((10,)),
            dma((10,)),
        ],
        compiler_params=pltpu.CompilerParams(vmem_limit_bytes=60 << 20),
        name="finish",
    )(branch, grads, sums)
    return (branch_rows[None, None], grads[None, None], weight_grad)


def solution(mesh):
    in_specs = (
        P("dp", "fsdp", None, None, None),
        P("fsdp", None),
        P(),
        P("dp", "fsdp", None, None),
        P(),
        P(),
        P(),
    )
    out_specs = (P("dp", "fsdp", None, None), P("dp", "fsdp", None, None, None), P("fsdp", None))
    return jax.shard_map(
        per_device, mesh=mesh, in_specs=in_specs, out_specs=out_specs, check_vma=False
    )
```

```python
import math

import jax
import jax.numpy as jnp
from jax import lax
from jax.experimental import pallas as pl
from jax.experimental.pallas import tpu as pltpu
from jax.sharding import PartitionSpec as P

HEADS = 13
HEAD = 128
WIDTH = HEADS * HEAD
D = 3200
IMGS = 8
MAXP = 64
OWN = 320
SHARD = 200
PADDED = 208
HALF = 8 * PADDED
BLOCK = 896
SECOND = WIDTH - BLOCK
PARTS = ((0, BLOCK), (BLOCK, WIDTH))
CUT = 96
PIECE, STRIDE = 64, 48
MASKED = -1e30
TURNS = 0o06725341
MESH = pl.DeviceIdType.MESH
INV_SCALE = 1.0 / math.sqrt(HEAD)
F32 = jnp.float32
BF16 = jnp.bfloat16

NN = (((1,), (0,)), ((), ()))
NT = (((1,), (1,)), ((), ()))
TN = (((0,), (0,)), ((), ()))


def mm(a, b, dims=NN):
    return lax.dot_general(a, b, dims, preferred_element_type=F32)


def two_heads(rows):
    none = jnp.zeros((MAXP, HEAD), BF16)
    upper = jnp.concatenate([rows[:, :HEAD], none], axis=1)
    lower = jnp.concatenate([none, rows[:, HEAD:]], axis=1)
    return jnp.concatenate([upper, lower], axis=0)


def stacked(rows):
    return two_heads(rows) if rows.shape[1] > HEAD else rows


def side_by_side(product):
    if product.shape[0] == MAXP:
        return product
    return jnp.concatenate([product[:MAXP, :HEAD], product[MAXP:, HEAD:]], axis=1)


def unit_columns(unit):
    first = 2 * unit - (unit > 3)
    return slice(first * HEAD, (first + 2 - (unit == 3)) * HEAD)


def by_columns(body, first=0, last=WIDTH):
    whole = (last - first) // 256

    @pl.loop(0, whole)
    def _(n):
        body(pl.multiple_of(first + n * 256, 128), 256)

    if (last - first) % 256:
        body(first + whole * 256, (last - first) % 256)


def spread_tile(tile):
    first = tile * 128
    group = first // PADDED
    inside = first % PADDED
    start = lax.min((group * SHARD + lax.min(inside, SHARD)) // 128, D // 128 - 2)
    place = first + lax.broadcasted_iota(jnp.int32, (256, 128), 1)
    source = start * 128 + lax.broadcasted_iota(jnp.int32, (256, 128), 0)
    groups = group + (place >= (group + 1) * PADDED).astype(jnp.int32)
    local = place - groups * PADDED
    hit = (source == groups * SHARD + local) & (local < SHARD)
    return start * 128, jnp.where(hit, 1.0, 0.0).astype(BF16)


def compact_tile(tile):
    first = tile * 128
    group = first // SHARD
    start = lax.min((first + group * (PADDED - SHARD)) // 128, 2 * HALF // 128 - 3)
    place = first + lax.broadcasted_iota(jnp.int32, (384, 128), 1)
    source = start * 128 + lax.broadcasted_iota(jnp.int32, (384, 128), 0)
    groups = group + (place >= (group + 1) * SHARD).astype(jnp.int32)
    hit = source == place + groups * (PADDED - SHARD)
    return start * 128, jnp.where(hit, 1.0, 0.0).astype(BF16)


def fused(
    plan, counts, offsets, shard_hbm, qkv_hbm, grad_hbm, scale,
    branch_hbm, qkv_grad_hbm, final_hbm,
    meta, wv, wp, wh, qkv, sc, scale_parts, scale_pad, sp, sx, att_send, att_recv, aa, soft_keep,
    gh, relay, direct, total, relay2, direct2, summed, ysum, mixed, final,
    ga_own, ga_send, ga_recv, back_send, back_first, back_second, bx, bp,
    in_sem, w0s, w0r, w1s, w1r, w3s, w3r, a2s, a2r, cs, cr, g1s, g1r, g2s, g2r, ys, yr, fs, fr, b2s, b2r, out_sem,
):
    d = lax.axis_index("dp")
    f = lax.axis_index("fsdp")
    c = f % 2
    z = (f // 2) % 4
    yl = f // 8
    x = d // 2
    y = (d % 2) * 2 + yl

    def at(px, py, pz, pc):
        px, py, pz = (px + 4) % 4, (py + 4) % 4, (pz + 4) % 4
        return (px * 2 + py // 2, ((py % 2) * 4 + pz) * 2 + pc)

    def remote(src, dst, send, recv, dev):
        return pltpu.make_async_remote_copy(
            src_ref=src, dst_ref=dst, send_sem=send, recv_sem=recv, device_id=dev, device_id_type=MESH
        )

    partner = at(x, y, z, 1 - c)

    load_w = pltpu.make_async_copy(shard_hbm, wv, in_sem.at[0])
    load_q = pltpu.make_async_copy(qkv_hbm, qkv, in_sem.at[1])
    load_g = pltpu.make_async_copy(grad_hbm, sc, in_sem.at[2])
    load_w.start()
    load_q.start()
    load_g.start()

    barrier = pltpu.get_barrier_semaphore()
    peers = [at(x, y, z + 1, c), at(x, y, z - 1, c), partner]
    for place in range(1, 16):
        for core in range(2):
            peers.append(at(x + place % 4, y + place // 4, z, core))
    for peer in peers:
        pl.semaphore_signal(barrier, inc=1, device_id=peer, device_id_type=MESH)
    owner_of = [(d + 8 - plan[0, k, f]) % 8 for k in range(IMGS)]
    for k in range(IMGS):
        meta[2, k] = owner_of[k]
    image_offset, image_count = [], []
    for e in range(8):
        slot, image = 0, 0
        for k in range(1, IMGS):
            slot = jnp.where(owner_of[k] == e, k, slot)
            image = jnp.where(plan[d, k, f] == e, k, image)
        meta[0, e] = slot
        meta[1, e] = counts[e, slot, f]
        image_offset.append(offsets[d, image, f])
        image_count.append(counts[d, image, f])
    load_w.wait()
    wp[0:192, :] = wv[0:192, :]
    wp[192:208, :] = jnp.concatenate(
        [wv[192:200, :].astype(F32), jnp.zeros((8, WIDTH), F32)], axis=0
    ).astype(BF16)
    pl.semaphore_wait(barrier, len(peers))

    def w_rows(pz, k):
        return wh.at[pl.ds(pl.multiple_of((((pz + 4) % 4) * 2 + k) * PADDED, 16), PADDED), :]

    w_y = remote(wp, w_rows(z, c), w0s.at[0], w0r.at[c], at(x, y + 1 - 2 * c, z, yl))
    w_c = remote(wp, w_rows(z, c), w0s.at[1], w0r.at[c], partner)
    w_l = pltpu.make_async_copy(wp, w_rows(z, c), w0s.at[1])
    w_y.start()

    @pl.when(c == yl)
    def _():
        w_l.start()

    @pl.when(c != yl)
    def _():
        w_c.start()

    load_q.wait()

    def partner_at(i, sign=1):
        n = TURNS // 8**i % 8 if isinstance(i, int) else lax.div(TURNS, lax.shift_left(1, 3 * i)) % 8
        return ((x + sign * (n % 4) + 4) % 4) * 2 + (d + n // 4) % 2

    def att_copy(i):
        owner = partner_at(i)
        return remote(att_send.at[owner], att_recv.at[d], a2s.at[i], a2r.at[i], (owner, f))

    @pl.loop(0, IMGS)
    def _(i):
        owner = partner_at(i)
        slot = meta[0, owner]
        count = meta[1, owner]
        for units in ((0, 1, 2, 3), (4, 5, 6)):
            scores = []
            for u in units:
                cols = unit_columns(u)
                q = qkv[slot, :, cols]
                k = qkv[slot, :, WIDTH + cols.start : WIDTH + cols.stop]
                scores.append(mm(k, stacked(q), NT) * INV_SCALE)
            softs = []
            for u, s in zip(units, scores):
                s = jnp.where(lax.broadcasted_iota(jnp.int32, s.shape, 0) < count, s, MASKED)
                e = jnp.exp(s - jnp.max(s, axis=0, keepdims=True))
                soft = e * (1.0 / jnp.sum(e, axis=0, keepdims=True))
                soft_keep[owner, u, :, : s.shape[1]] = soft
                softs.append(soft.astype(BF16))
            for u, soft in zip(units, softs):
                cols = unit_columns(u)
                v = qkv[slot, :, 2 * WIDTH + cols.start : 2 * WIDTH + cols.stop]
                att_send[owner, :, cols] = side_by_side(mm(soft, v, TN)).astype(BF16)

        @pl.when(i < 7)
        def _():
            att_copy(i).start()

    att_recv[d] = att_send[d]

    for k in range(2):
        @pl.when((c != yl) | (c != k))
        def _():
            remote(wp, w_rows(z, k), w0s.at[0], w0r.at[k], partner).wait_recv()

    @pl.when(c == yl)
    def _():
        w_l.wait()

    up, down = at(x, y, z + 1, c), at(x, y, z - 1, c)
    w1 = [
        remote(w_rows(z, 0), w_rows(z, 0), w1s.at[0], w1r.at[0], up),
        remote(w_rows(z, 1), w_rows(z, 1), w1s.at[1], w1r.at[1], down),
        remote(w_rows(z, 1), w_rows(z, 1), w1s.at[2], w1r.at[2], up),
        remote(w_rows(z, 0), w_rows(z, 0), w1s.at[3], w1r.at[3], down),
    ]

    @pl.when(c == yl)
    def _():
        for copy in w1:
            copy.start()

    w2 = [
        remote(w_rows(z - 1, 0), w_rows(z - 1, 0), w1s.at[4], w1r.at[4], up),
        remote(w_rows(z + 1, 1), w_rows(z + 1, 1), w1s.at[5], w1r.at[5], down),
    ]

    load_g.wait()

    scale_row = scale[...].reshape(1, D)

    @pl.loop(0, OWN // 16)
    def _(r):
        rows = pl.ds(pl.multiple_of(r * 16, 16), 16)
        sc[rows, :] = (sc[rows, :].astype(F32) * scale_row).astype(BF16)

    high_part = scale_row.astype(BF16).astype(F32)
    mid_part = (scale_row - high_part).astype(BF16).astype(F32)
    low_part = scale_row - high_part - mid_part
    part = lax.broadcasted_iota(jnp.int32, (16, D), 0)
    scale_parts[...] = jnp.where(
        part == 0, high_part, jnp.where(part == 1, mid_part, jnp.where(part == 2, low_part, 0.0))
    ).astype(BF16)

    own_rows = pl.ds(pl.multiple_of(c * OWN, 16), OWN)
    other_rows = pl.ds(pl.multiple_of((1 - c) * OWN, 16), OWN)

    @pl.loop(0, HALF // 128, unroll=True)
    def _(t):
        start, pick = spread_tile((1 - c) * (HALF // 128) + t)
        window = sc[:, pl.ds(pl.multiple_of(start, 128), 256)]
        sx[:, pl.ds(pl.multiple_of(t * 128, 128), 128)] = mm(window, pick).astype(BF16)

    send_sx = remote(sx, sp.at[own_rows, :], cs.at[0], cr.at[0], partner)
    send_sx.start()

    @pl.loop(0, HALF // 128, unroll=True)
    def _(t):
        start, pick = spread_tile(c * (HALF // 128) + t)
        window = sc[:, pl.ds(pl.multiple_of(start, 128), 256)]
        there = pl.ds(pl.multiple_of(t * 128, 128), 128)
        sp[own_rows, there] = mm(window, pick).astype(BF16)
        parts = mm(scale_parts[:, pl.ds(pl.multiple_of(start, 128), 256)], pick)
        scale_pad[:, there] = jnp.sum(parts, axis=0, keepdims=True)

    def w_on(step, k):
        pz = z + (1, -1, 2)[step]
        sem = 2 * step + k
        return remote(
            w_rows(pz, k), w_rows(pz, k), w3s.at[sem], w3r.at[sem], at(x, y + 1 - 2 * k, z, c)
        )

    @pl.when(c == yl)
    def _():
        w1[0].wait_recv()
        w2[0].start()
        w_on(1, 0).start()
        w1[1].wait_recv()
        w2[1].start()
        w_on(0, 1).start()
        w1[2].wait_recv()
        w_on(1, 1).start()
        w1[3].wait_recv()
        w_on(0, 0).start()
        for k in range(2):
            w2[k].wait_recv()
            w_on(2, k).start()

    for i in range(7):
        source = partner_at(i, -1)
        remote(att_send.at[source], att_recv.at[source], a2s.at[i], a2r.at[i], partner).wait_recv()
    lane = lax.broadcasted_iota(jnp.int32, (1, IMGS * MAXP), 1)
    source_row = jnp.full((1, IMGS * MAXP), -1, jnp.int32)
    for n in range(8):
        inside = lane - n * MAXP
        source_row = jnp.where(
            (inside >= 0) & (inside < image_count[n]), inside + image_offset[n], source_row
        )
    pack = jnp.where(
        lax.broadcasted_iota(jnp.int32, (OWN, IMGS * MAXP), 0) == source_row, 1.0, 0.0
    ).astype(BF16)

    def pack_columns(start, size):
        got = att_recv[:, :, pl.ds(start, size)].reshape(IMGS * MAXP, size)
        aa[own_rows, pl.ds(start, size)] = mm(pack, got).astype(BF16)

    by_columns(pack_columns)
    send_aa = remote(aa.at[own_rows, :], aa.at[own_rows, :], cs.at[1], cr.at[1], partner)
    send_aa.start()
    remote(sx, sp.at[other_rows, :], cs.at[0], cr.at[0], partner).wait_recv()
    remote(aa.at[other_rows, :], aa.at[other_rows, :], cs.at[1], cr.at[1], partner).wait_recv()

    def block(first, second):
        first, second = (first + 4) % 4, (second + 4) % 4
        pz = first * (1 - c) + second * c
        kh = second * (1 - c) + first * c
        return kh % 2, pl.ds(pl.multiple_of((pz * 2 + kh // 2) * PADDED, 16), PADDED)

    p1 = z * (1 - c) + x * c
    p2 = y * (1 - c) + z * c
    right1, left1 = at(x + c, y, z + 1 - c, c), at(x - c, y, z - 1 + c, c)
    right2, left2 = at(x, y + 1 - c, z + c, c), at(x, y - 1 + c, z - c, c)

    def g1(first, j, dst, sem, dev):
        h, rows = block(first, j)
        return remote(gh.at[h, rows, :], dst, g1s.at[sem], g1r.at[sem], dev)

    s1 = [g1(p1 + 2, j, relay.at[0, j], j, right1) for j in (0, 1)]
    s1 += [g1(p1 + 2, j, relay.at[1, j - 2], j, left1) for j in (2, 3)]
    s1 += [g1(p1 + 1, j, direct.at[0, j], 4 + j, right1) for j in (2, 3)]
    s1 += [g1(p1 - 1, j, direct.at[1, j], 8 + j, left1) for j in (0, 1)]

    def weight_columns(h):
        cols = pl.ds(pl.multiple_of(h * SECOND, 128), BLOCK)

        @pl.loop(0, HALF // 128)
        def _(t):
            rows = pl.ds(pl.multiple_of(t * 128, 128), 128)
            gh[h, rows, :] = mm(sp[:, rows], aa[:, cols], TN).astype(BF16)

    weight_columns(0)
    weight_columns(1)
    first_sends = [s1[n] for n in (0, 2, 1, 3, 4, 6, 5, 7)]

    for copy in first_sends:
        copy.start()
    r1 = [g1(p1 + 1, j, direct.at[0, j], 4 + j, right1) for j in (0, 1)]
    r1 += [g1(p1 - 1, j, direct.at[1, j], 8 + j, left1) for j in (2, 3)]

    def add_rows(rows, body):
        @pl.loop(0, rows // 16)
        def _(r):
            body(pl.multiple_of(r * 16, 16))

    @pl.when(c != yl)
    def _():
        for step in range(3):
            for k in range(2):
                w_on(step, k).wait_recv()

    def grad_columns(start, size):
        cols = pl.ds(start, size)
        ga_send[:, cols] = mm(sp[other_rows, :], wh[:, cols])
        ga_own[:, cols] = mm(sp[own_rows, :], wh[:, cols])

    send_ga = []
    for n, (first, last) in enumerate(PARTS):
        by_columns(grad_columns, first, last)
        cols = pl.ds(first, last - first)
        send_ga.append(
            remote(ga_send.at[:, cols], ga_recv.at[:, cols], cs.at[2 + n], cr.at[2 + n], partner)
        )
        send_ga[n].start()
    unpack = []
    for n in range(8):
        inside = lax.broadcasted_iota(jnp.int32, (MAXP, OWN), 0)
        column = lax.broadcasted_iota(jnp.int32, (MAXP, OWN), 1)
        hit = (inside < image_count[n]) & (column == inside + image_offset[n])
        unpack.append(jnp.where(hit, 1.0, 0.0).astype(BF16))
    unpack = jnp.concatenate(unpack, axis=0)

    def unpack_columns(start, size):
        cols = pl.ds(start, size)
        grad = (ga_own[:, cols] + ga_recv[:, cols]).astype(BF16)
        back_send[:, :, cols] = mm(unpack, grad).astype(BF16).reshape(IMGS, MAXP, size)

    back_parts = (back_first, back_second)

    def back_copy(i, n):
        loader = partner_at(i)
        cols = pl.ds(PARTS[n][0], PARTS[n][1] - PARTS[n][0])
        return remote(
            back_send.at[loader, :, cols], back_parts[n].at[d],
            b2s.at[7 * n + i], b2r.at[7 * n + i], (loader, f),
        )

    for n, j in enumerate((0, 2, 1, 3)):
        side, place = (0, p1 + 1) if j < 2 else (1, p1 - 1)
        s1[j].wait_recv()
        h, rows = block(place, j)
        base = rows.start

        def add_relay(r, h=h, base=base, side=side, j=j):
            here = pl.ds(pl.multiple_of(base + r, 16), 16)
            gh[h, here, :] = (
                gh[h, here, :].astype(F32) + relay[side, j % 2, pl.ds(r, 16), :].astype(F32)
            ).astype(BF16)

        add_rows(PADDED, add_relay)
        r1[j].start()

    for n in range(2):
        send_ga[n].wait_recv()
        by_columns(unpack_columns, *PARTS[n])
        for i in range(7):
            back_copy(i, n).start()
    for n in range(2):
        back_parts[n][d] = back_send[d, :, PARTS[n][0] : PARTS[n][1]]

    def project_rows(start, size):
        cols = pl.ds(start, size)
        bx[:, cols] = (scale_pad[:, cols] * mm(aa[...], wh[cols, :], NT)).astype(BF16)

    by_columns(project_rows)
    my_half = bp.at[:, pl.ds(pl.multiple_of(c * HALF, 128), HALF)]
    other_half = bp.at[:, pl.ds(pl.multiple_of((1 - c) * HALF, 128), HALF)]
    send_bx = remote(bx.at[other_rows, :], my_half, cs.at[4], cr.at[4], partner)
    send_bx.start()
    keep_bx = pltpu.make_async_copy(bx.at[own_rows, :], my_half, out_sem.at[10])
    keep_bx.start()

    for j in range(4):
        (s1[4 + j - 2] if j >= 2 else r1[j]).wait_recv()
        (s1[6 + j] if j < 2 else r1[j]).wait_recv()
        h, rows = block(p1, j)
        base = rows.start

        def add_first(r, h=h, base=base, j=j):
            here = pl.ds(r, 16)
            total[j, here, :] = (
                gh[h, pl.ds(pl.multiple_of(base + r, 16), 16), :].astype(F32)
                + direct[0, j, here, :].astype(F32)
                + direct[1, j, here, :].astype(F32)
            ).astype(BF16)

        add_rows(PADDED, add_first)

    low, high = pl.ds(0, CUT), pl.ds(CUT, PADDED - CUT)

    def g2(place, rows, dst, sem, dev):
        return remote(total.at[(place + 4) % 4, rows, :], dst, g2s.at[sem], g2r.at[sem], dev)

    s2 = [
        g2(p2 + 2, low, relay2.at[low, :], 0, right2),
        g2(p2 + 2, high, relay2.at[high, :], 1, left2),
        g2(p2 + 1, high, direct2.at[0, high, :], 2, right2),
        g2(p2 - 1, low, direct2.at[1, low, :], 3, left2),
    ]
    r2 = [
        g2(p2 + 1, low, direct2.at[0, low, :], 4, right2),
        g2(p2 - 1, high, direct2.at[1, high, :], 5, left2),
    ]
    for copy in s2:
        copy.start()

    for side in range(2):
        s2[side].wait_recv()
        place = (p2 + 1 if side == 0 else p2 + 3) % 4
        offset, rows = (0, CUT) if side == 0 else (CUT, PADDED - CUT)

        def add_relay2(r, place=place, offset=offset):
            here = pl.ds(pl.multiple_of(offset + r, 16), 16)
            total[place, here, :] = (
                total[place, here, :].astype(F32) + relay2[here, :].astype(F32)
            ).astype(BF16)

        add_rows(rows, add_relay2)
        r2[side].start()

    for copy in (s2[2], s2[3], r2[0], r2[1]):
        copy.wait_recv()

    def add_second(r):
        here = pl.ds(r, 16)
        summed[here, :] = (
            total[p2, here, :].astype(F32)
            + direct2[0, here, :].astype(F32)
            + direct2[1, here, :].astype(F32)
        ).astype(BF16)

    add_rows(PADDED, add_second)

    p3 = x * (1 - c) + y * c

    def piece(place):
        return pl.ds(pl.multiple_of((place + 4) % 4 * STRIDE, 16), PIECE)

    s3 = [
        remote(
            summed.at[piece(p3 + m), :], ysum.at[n], ys.at[n], yr.at[n],
            at(x + (1 - c) * m, y + c * m, z, c),
        )
        for n, m in enumerate((1, 3, 2))
    ]
    for copy in s3:
        copy.start()

    keep_bx.wait()
    remote(bx.at[other_rows, :], other_half, cs.at[4], cr.at[4], partner).wait_recv()

    @pl.loop(0, D // 128, unroll=5)
    def _(t):
        start, pick = compact_tile(t)
        window = bp[:, pl.ds(pl.multiple_of(start, 128), 384)]
        sc[:, pl.ds(pl.multiple_of(t * 128, 128), 128)] = mm(window, pick).astype(BF16)

    store_branch = pltpu.make_async_copy(sc, branch_hbm, out_sem.at[8])
    store_branch.start()

    for copy in s3:
        copy.wait_recv()

    @pl.loop(0, PIECE // 16)
    def _(r):
        here = pl.ds(pl.multiple_of(r * 16, 16), 16)
        there = pl.ds(pl.multiple_of(p3 * STRIDE + r * 16, 16), 16)
        mixed[here, :] = (
            summed[there, :].astype(F32)
            + ysum[0, here, :].astype(F32)
            + ysum[1, here, :].astype(F32)
            + ysum[2, here, :].astype(F32)
        ).astype(BF16)

    kept = y * (1 - c) + x * c
    keeper = kept // 2
    column = kept % 2
    mine = (c == yl) & (keeper == c)

    def for_spread(act):
        for n in (1, 3, 2, 0):
            for m in range(2):
                copy = remote(
                    mixed, final.at[column, p3], fs.at[2 * n + m], fr.at[column * 4 + p3],
                    at(x + n, c + 2 * m, z, keeper),
                )
                if n:
                    act(copy)
                else:
                    @pl.when(jnp.logical_not((y == c + 2 * m) & (keeper == c)))
                    def _():
                        act(copy)

    for_spread(lambda copy: copy.start())

    def backward(slot, groups):
        owner = meta[2, slot]
        for units in groups:
            stages = []
            for u in units:
                cols = unit_columns(u)
                v = qkv[slot, :, 2 * WIDTH + cols.start : 2 * WIDTH + cols.stop]
                skip, got = (0, back_first) if u < 4 else (BLOCK, back_second)
                go = stacked(got[owner, :, cols.start - skip : cols.stop - skip])
                soft = soft_keep[owner, u, :, : go.shape[0]]
                stages.append((u, go, soft, mm(v, go, NT)))
            for u, go, soft, grad_soft in stages:
                cols = unit_columns(u)
                kcols = slice(WIDTH + cols.start, WIDTH + cols.stop)
                vcols = slice(2 * WIDTH + cols.start, 2 * WIDTH + cols.stop)
                q, k = stacked(qkv[slot, :, cols]), qkv[slot, :, kcols]
                delta = jnp.sum(soft * grad_soft, axis=0, keepdims=True)
                gs = (soft * (grad_soft - delta)).astype(BF16)
                grad_v = mm(soft.astype(BF16), go)
                grad_k = mm(gs, q) * INV_SCALE
                grad_q = side_by_side(mm(gs, k, TN)) * INV_SCALE
                qkv[slot, :, vcols] = grad_v.astype(BF16)
                qkv[slot, :, kcols] = grad_k.astype(BF16)
                qkv[slot, :, cols] = grad_q.astype(BF16)

    def store_slot(slot):
        return pltpu.make_async_copy(qkv.at[slot], qkv_grad_hbm.at[slot], out_sem.at[slot])

    def wait_back(n):
        for i in range(7):
            source = partner_at(i, -1)
            cols = pl.ds(PARTS[n][0], PARTS[n][1] - PARTS[n][0])
            remote(
                back_send.at[source, :, cols], back_parts[n].at[source],
                b2s.at[7 * n + i], b2r.at[7 * n + i], partner,
            ).wait_recv()

    wait_back(0)

    @pl.loop(0, IMGS)
    def _(slot):
        backward(slot, ((0, 1), (2, 3)))

    wait_back(1)

    @pl.loop(0, IMGS)
    def _(slot):
        backward(slot, ((4, 5, 6),))
        store_slot(slot).start()

    for n in range(2):
        for q in range(4):
            own = mine & (column == n) & (p3 == q)

            @pl.when(own)
            def _():
                final[n, q] = mixed[...]

            @pl.when(jnp.logical_not(own))
            def _():
                remote(mixed, final.at[n, q], fs.at[0], fr.at[n * 4 + q], partner).wait_recv()

    store_w = pltpu.make_async_copy(final, final_hbm, out_sem.at[9])
    store_w.start()
    w_y.wait_send()

    @pl.when(c != yl)
    def _():
        w_c.wait_send()

    @pl.when(c == yl)
    def _():
        for copy in (*w1, *w2):
            copy.wait_send()
        for step in range(3):
            for k in range(2):
                w_on(step, k).wait_send()

    for_spread(lambda copy: copy.wait_send())
    for i in range(7):
        att_copy(i).wait_send()
        back_copy(i, 0).wait_send()
        back_copy(i, 1).wait_send()
    for copy in (send_sx, send_aa, *send_ga, send_bx, *s1, *r1, *s2, *r2, *s3):
        copy.wait_send()
    for slot in range(IMGS):
        store_slot(slot).wait()
    store_branch.wait()
    store_w.wait()


def finish(
    branch_hbm, grads_hbm, sums_hbm, branch_out, grads_out, weight_out,
    branch, grads, sums, weight, in_sem, out_sem,
):
    load_branch = pltpu.make_async_copy(branch_hbm, branch, in_sem.at[8])
    load_sums = pltpu.make_async_copy(sums_hbm, sums, in_sem.at[9])
    loads = [pltpu.make_async_copy(grads_hbm.at[k], grads.at[k], in_sem.at[k]) for k in range(IMGS)]
    stores = [pltpu.make_async_copy(grads.at[k], grads_out.at[k], out_sem.at[k]) for k in range(IMGS)]
    store_branch = pltpu.make_async_copy(branch, branch_out, out_sem.at[8])
    store_weight = pltpu.make_async_copy(weight, weight_out, out_sem.at[9])
    load_sums.start()
    for load in loads:
        load.start()
    load_branch.start()
    load_sums.wait()
    for q in range(4):
        size = STRIDE if q < 3 else SHARD - 3 * STRIDE
        here = slice(q * STRIDE, q * STRIDE + size)
        weight[here, :BLOCK] = sums[0, q].astype(F32)[:size]
        weight[here, SECOND:] = sums[1, q].astype(F32)[:size]
    store_weight.start()
    for k in range(IMGS):
        loads[k].wait()
        stores[k].start()
    load_branch.wait()
    store_branch.start()
    for store in (store_weight, *stores, store_branch):
        store.wait()


def per_device(
    qkv_rows, proj_weight, layer_scale, out_grad, patch_counts, loader_plan, row_offsets
):
    tables = [jnp.swapaxes(table, 1, 2) for table in (loader_plan, patch_counts, row_offsets)]
    vmem = pl.BlockSpec(memory_space=pltpu.VMEM)
    smem = pl.BlockSpec(memory_space=pltpu.SMEM)
    hbm = pl.BlockSpec(memory_space=pl.ANY)
    dma = pltpu.SemaphoreType.DMA
    rows = (PADDED, BLOCK)
    grads_shape = jax.ShapeDtypeStruct((IMGS, MAXP, 3 * WIDTH), BF16)
    branch, grads, sums = pl.pallas_call(
        fused,
        out_shape=(
            jax.ShapeDtypeStruct((OWN, D), BF16),
            grads_shape,
            jax.ShapeDtypeStruct((2, 4, PIECE, BLOCK), BF16),
        ),
        in_specs=[smem, smem, smem, hbm, hbm, hbm, vmem],
        out_specs=(hbm, hbm, hbm),
        scratch_shapes=[
            pltpu.SMEM((3, 8), jnp.int32),
            pltpu.VMEM((SHARD, WIDTH), BF16),
            pltpu.VMEM((PADDED, WIDTH), BF16),
            pltpu.VMEM((HALF, WIDTH), BF16),
            pltpu.VMEM((IMGS, MAXP, 3 * WIDTH), BF16),
            pltpu.VMEM((OWN, D), BF16),
            pltpu.VMEM((16, D), BF16),
            pltpu.VMEM((1, HALF), F32),
            pltpu.VMEM((2 * OWN, HALF), BF16),
            pltpu.VMEM((OWN, HALF), BF16),
            pltpu.VMEM((IMGS, MAXP, WIDTH), BF16),
            pltpu.VMEM((IMGS, MAXP, WIDTH), BF16),
            pltpu.VMEM((2 * OWN, WIDTH), BF16),
            pltpu.VMEM((IMGS, (HEADS + 1) // 2, MAXP, 2 * MAXP), F32),
            pltpu.VMEM((2, HALF, BLOCK), BF16),
            pltpu.VMEM((2, 2, *rows), BF16),
            pltpu.VMEM((2, 4, *rows), BF16),
            pltpu.VMEM((4, *rows), BF16),
            pltpu.VMEM(rows, BF16),
            pltpu.VMEM((2, *rows), BF16),
            pltpu.VMEM(rows, BF16),
            pltpu.VMEM((3, PIECE, BLOCK), BF16),
            pltpu.VMEM((PIECE, BLOCK), BF16),
            pltpu.VMEM((2, 4, PIECE, BLOCK), BF16),
            pltpu.VMEM((OWN, WIDTH), F32),
            pltpu.VMEM((OWN, WIDTH), F32),
            pltpu.VMEM((OWN, WIDTH), F32),
            pltpu.VMEM((IMGS, MAXP, WIDTH), BF16),
            pltpu.VMEM((IMGS, MAXP, BLOCK), BF16),
            pltpu.VMEM((IMGS, MAXP, WIDTH - BLOCK), BF16),
            pltpu.VMEM((2 * OWN, HALF), BF16),
            pltpu.VMEM((OWN, 2 * HALF), BF16),
            dma((3,)),
            dma((2,)), dma((2,)),
            dma((6,)), dma((6,)),
            dma((6,)), dma((6,)),
            dma((7,)), dma((7,)),
            dma((5,)), dma((5,)),
            dma((12,)), dma((12,)),
            dma((6,)), dma((6,)),
            dma((3,)), dma((3,)),
            dma((8,)), dma((8,)),
            dma((14,)), dma((14,)),
            dma((11,)),
        ],
        compiler_params=pltpu.CompilerParams(
            collective_id=0, has_side_effects=True, vmem_limit_bytes=62 << 20
        ),
        cost_estimate=pl.CostEstimate(
            flops=13_000_000_000, bytes_accessed=20_000_000, transcendentals=500_000
        ),
        name="attention_sublayer",
    )(
        *tables,
        proj_weight,
        qkv_rows[0, 0],
        out_grad[0, 0],
        layer_scale,
    )
    branch_rows, grads, weight_grad = pl.pallas_call(
        finish,
        out_shape=(
            jax.ShapeDtypeStruct((OWN, D), BF16),
            grads_shape,
            jax.ShapeDtypeStruct((SHARD, WIDTH), F32),
        ),
        in_specs=[hbm, hbm, hbm],
        out_specs=(hbm, hbm, hbm),
        scratch_shapes=[
            pltpu.VMEM((OWN, D), BF16),
            pltpu.VMEM((IMGS, MAXP, 3 * WIDTH), BF16),
            pltpu.VMEM((2, 4, PIECE, BLOCK), BF16),
            pltpu.VMEM((SHARD, WIDTH), F32),
            dma((10,)),
            dma((10,)),
        ],
        compiler_params=pltpu.CompilerParams(vmem_limit_bytes=60 << 20),
        name="finish",
    )(branch, grads, sums)
    return (branch_rows[None, None], grads[None, None], weight_grad)


def solution(mesh):
    in_specs = (
        P("dp", "fsdp", None, None, None),
        P("fsdp", None),
        P(),
        P("dp", "fsdp", None, None),
        P(),
        P(),
        P(),
    )
    out_specs = (P("dp", "fsdp", None, None), P("dp", "fsdp", None, None, None), P("fsdp", None))
    return jax.shard_map(
        per_device, mesh=mesh, in_specs=in_specs, out_specs=out_specs, check_vma=False
    )
```
